32 devices in a mesh: row: 4 (over y, x), col: 8 (over z, core).
Axes of the slice: x: 2, y: 2, z: 4, core: 2. Of those that a mesh axis runs over, the one named last changes fastest.
Arguments:
- grad_out: bfloat16 [4096, 512], P(('row', 'col'))
- relu_mask: int32 [4096, 512], P(('row', 'col')), may hold values 0 or 1
- aggregated: bfloat16 [4096, 512], P(('row', 'col')), may hold values from -6 to 6
- weight: bfloat16 [512, 512], replicated, may hold values from -0.25 to 0.25
- adj_blocks: bfloat16 [4, 8, 5, 128, 128], P('row', 'col'), may hold values from 0 to 0.11867817
- block_pos: int32 [4, 8, 5], P('row', 'col'), may hold values from 0 to 31, as said below
- block_live: int32 [4, 8], P('row', 'col'), may hold values from 1 to 5, as said below
Outputs:
- grad_input: bfloat16 [8, 512, 512], P('col', 'row')
- grad_weight: float32 [512, 512], replicated
- grad_bias: float32 [512], replicated
The draws below stay inside these ranges and needn't reach their ends.
Inputs may be any that keep to these rules, and one draw needn't show every extreme that they name: `block_pos`: within one tile the 5 slots name different positions; position p is block row p // 4, block column p % 4. `block_live`: some tile uses all 5 slots.
All inputs are finite; a program needn't handle non-finite values. No bound on the sum of `relu_mask` on one device may be relied on, other than what follows from the above.
Results may differ from the reference program's by a relative error of at most 0.005.
Values may be sent and summed in bfloat16 or wider, within the bound.
A program may use at most 64 MiB of HBM per device.

```python
import math
import jax
import jax.numpy as jnp
from jax import lax

FEAT = 512
BLK = 128
NODES = 4096
TBR = 8
TBC = 4
CAP = 5
N_ROW = 4
N_COL = 8


def draw_grad_out(key, part):
    first_key, second_key = jax.random.split(key, 2)
    order = jnp.arange(NODES, dtype=jnp.float32)
    rising = 1.0 + 2.0 * order / max(NODES - 1, 1)
    rough = jnp.exp(jax.random.uniform(second_key, (NODES,), jnp.float32, math.log(0.15), math.log(1.5)))
    values = jax.random.normal(first_key, (NODES, FEAT), jnp.float32)
    return (values * (rising * rough)[:, None]).astype(jnp.bfloat16)


def draw_adj_blocks(key, part):
    first_key = jax.random.fold_in(jax.random.fold_in(key, 7), 0)
    fan_in = BLK * CAP * N_ROW // (3 * TBC)
    top = math.sqrt(3.0 / fan_in) * 0.99
    shape = (N_ROW, N_COL, CAP, BLK, BLK)
    values = jax.random.uniform(first_key, shape, jnp.float32, 0.0, 1.0) * top
    return values.astype(jnp.bfloat16)


def draw_block_pos(key, part):
    position_count = TBR * TBC
    tile_keys = jax.random.split(key, N_ROW * N_COL)
    chosen = jax.vmap(lambda item: jax.random.permutation(item, position_count)[:CAP])(tile_keys).astype(jnp.int32)
    holder = jnp.any(chosen[0] == position_count - 1)
    first_tile = jnp.where(holder, chosen[0], chosen[0].at[0].set(position_count - 1))
    chosen = chosen.at[0].set(first_tile)
    return chosen.reshape(N_ROW, N_COL, CAP)


def draw_block_live(key, part):
    first_key, second_key = jax.random.split(key)
    sampled = jax.random.randint(first_key, (N_ROW * N_COL,), 1, CAP + 1)
    counts = jnp.maximum(1, sampled * sampled // CAP)
    fullest = jax.random.randint(second_key, (), 0, N_ROW * N_COL)
    counts = jnp.where(jnp.arange(N_ROW * N_COL) == fullest, CAP, counts)
    return counts.astype(jnp.int32).reshape(N_ROW, N_COL)


def set_ends(entries, rng, low, largest):
    longest = entries.shape.index(max(entries.shape))
    spots = []
    for shift in (0, 1):
        where = [jax.random.randint(jax.random.fold_in(rng, axis), (), 0, length) for axis, length in enumerate(entries.shape)]
        where[longest] = (where[longest] + shift) % entries.shape[longest]
        spots.append(tuple(where))
    return entries.at[spots[0]].set(low).at[spots[1]].set(largest)


def shard_levels(rng, dims, cuts, least, largest):
    def one(dim, parts):
        draws = jax.random.uniform(jax.random.fold_in(jax.random.fold_in(rng, 6), dim), (parts,), jnp.float32, least / len(cuts), largest / len(cuts))
        return jnp.repeat(jnp.exp(draws), dims[dim] // parts).reshape((-1,) + (1,) * (len(dims) - dim - 1))

    factor_of = one(*cuts[0])
    for cut in cuts[1:]:
        factor_of = factor_of * one(*cut)
    return factor_of


def scatter_about(stream_key, dims, deviation, reach, shards=(), kind=jnp.bfloat16):
    level = shard_levels(stream_key, dims, shards, -0.22, 0.18) if shards else 1.0
    entries = jax.random.normal(stream_key, dims, jnp.float32) * deviation * level
    return jnp.minimum(jnp.maximum(entries, -reach), reach).astype(kind)


def setup_inputs(seed: int = 0) -> dict:
    key_list = jax.random.split(jax.random.key(seed), 8)
    return {
        "grad_out": draw_grad_out(jax.random.fold_in(key_list[7], 71), 0),
        "relu_mask": set_ends((jax.random.randint(key_list[1], (NODES, FEAT), 0, 2) < 1).astype(jnp.int32), jax.random.fold_in(key_list[1], 1), 0, 1),
        "aggregated": scatter_about(key_list[2], (NODES, FEAT), 1.0, 6.0, ((0, 32),)),
        "weight": scatter_about(key_list[3], (FEAT, FEAT), FEAT ** -0.5, 0.25),
        "adj_blocks": draw_adj_blocks(jax.random.fold_in(key_list[7], 71), 0),
        "block_pos": draw_block_pos(jax.random.fold_in(key_list[7], 71), 0),
        "block_live": draw_block_live(jax.random.fold_in(key_list[7], 71), 0),
    }


def reference(grad_out, relu_mask, aggregated, weight, adj_blocks, block_pos, block_live):
    grad_pre = grad_out * relu_mask.astype(jnp.bfloat16)
    gradient_row_slice = jnp.dot(grad_pre, weight.T, preferred_element_type=jnp.float32).astype(jnp.bfloat16)
    tile_height = NODES // N_ROW

    def one_column(tile_col):

        def add_tile(running_total, tile_row):
            stacked_tiles = lax.dynamic_slice_in_dim(gradient_row_slice, tile_row * tile_height, tile_height, 0)
            stacked_tiles = stacked_tiles.reshape(TBR, BLK, FEAT).astype(jnp.float32)
            positions = block_pos[tile_row, tile_col]
            blocks = adj_blocks[tile_row, tile_col].astype(jnp.float32)
            picked = stacked_tiles[positions // TBC]
            alive = (jnp.arange(CAP, dtype=jnp.int32) < block_live[tile_row, tile_col]).astype(jnp.float32)
            partial_products = jnp.einsum('kab,kaf->kbf', blocks, picked) * alive[:, None, None]
            insert_position = ((positions % TBC)[:, None] == jnp.arange(TBC, dtype=jnp.int32)[None, :]).astype(jnp.float32)
            return (running_total + jnp.einsum('lj,lsu->jsu', insert_position, partial_products), None)
        start_sum = jnp.zeros((TBC, BLK, FEAT), jnp.float32)
        running_total, _ = lax.scan(add_tile, start_sum, jnp.arange(N_ROW, dtype=jnp.int32))
        return running_total.reshape(TBC * BLK, FEAT)
    full_input = lax.map(one_column, jnp.arange(N_COL, dtype=jnp.int32))
    grad_input = full_input.astype(jnp.bfloat16)
    factor = 1.0 / math.sqrt(NODES)
    grad_weight = jnp.einsum('nf,ng->fg', aggregated.astype(jnp.float32), grad_pre.astype(jnp.float32)) * factor
    grad_bias = lax.optimization_barrier(jnp.sum(grad_pre.astype(jnp.float32), axis=0)) * factor
    return (grad_input, grad_weight, grad_bias)
```

```python
import functools
import math

import jax
import jax.numpy as jnp
from jax import lax
from jax.experimental import pallas as pl
from jax.experimental.pallas import tpu as pltpu
from jax.sharding import PartitionSpec as P

MESH = pl.DeviceIdType.MESH
BF = jnp.bfloat16
F32 = jnp.float32
TILE = 16


def dot0(a, b):
    return lax.dot_general(a, b, (((0,), (0,)), ((), ())), preferred_element_type=F32)


def kernel(cfg, go_ref, mask_ref, agg_ref, w_ref, blk_ref, pos_ref, live_ref,
           gi_ref, gw_ref, gb_ref, *scr):
    n_row, n_col, nch, cap, group, scatter = cfg
    n_z = n_col // 2
    gath = scr[:nch]
    lhs, cbuf, rbuf, asib, gpart, grecv, zsend, zrecv, gw = scr[nch:nch + 9]
    ag_s, ag_r, fw_s, fw_r, c_s, c_r, as_s, as_r, g_s, g_r, z_s, z_r, wz_s, wz_r, wr_s, wr_r, wf_s, wf_r = scr[nch + 9:]
    rows, feat = go_ref.shape
    fc = feat // nch
    blk = blk_ref.shape[-1]
    tbc = n_row * rows // blk
    half = feat // 2
    piece = half // n_row
    part = piece // n_z if scatter else piece
    me_r, me_c = lax.axis_index("row"), lax.axis_index("col")
    z, core = me_c // 2, me_c % 2
    sib = z * 2 + 1 - core
    sib_id = (me_r, sib)

    def row_id(d):
        return ((me_r + d) % n_row, me_c)

    def z_id(d):
        return (me_r, ((z + d) % n_z) * 2 + core)

    sent = []

    def send(src, dst, s, r, dev):
        c = pltpu.make_async_remote_copy(src_ref=src, dst_ref=dst, send_sem=s, recv_sem=r,
                                         device_id=dev, device_id_type=MESH)
        c.start()
        sent.append(c)
        return c

    barrier = pltpu.get_barrier_semaphore()
    peers = [sib_id] + [z_id(d) for d in range(1, n_z)] + [row_id(d) for d in range(1, n_row)]
    for p in peers:
        pl.semaphore_signal(barrier, inc=1, device_id=p, device_id_type=MESH)

    for ch in range(nch):
        cols = slice(ch * fc, (ch + 1) * fc)
        gath[ch][me_c] = go_ref[:, cols] * mask_ref[:, cols].astype(F32).astype(BF)

    pl.semaphore_wait(barrier, len(peers))

    sib_cp, z_cp = [], []
    other = pl.ds(pl.multiple_of((1 - core) * half, half), half)
    mine = pl.ds(pl.multiple_of(core * half, half), half)
    agg_cp = send(agg_ref.at[:, other], asib, as_s, as_r, sib_id)
    for ch in range(nch):
        own = gath[ch].at[me_c]
        sib_cp.append(send(own, own, ag_s.at[ch, 0], ag_r.at[ch, 0], sib_id))
        z_cp.append([send(own, own, ag_s.at[ch, d], ag_r.at[ch, d], z_id(d)) for d in range(1, n_z)])

    agg_cp.wait_recv()
    bias = jnp.zeros((1, feat), F32)
    sums = []
    for ch in range(nch):
        cols = slice(ch * fc, (ch + 1) * fc)
        sib_cp[ch].wait_recv()
        a, b = gath[ch][me_c], gath[ch][sib]
        g = dot0(agg_ref[:, mine], a) + dot0(asib[...], b)
        gpart[:, 0:piece, cols] = g.astype(BF).reshape(n_row, piece, fc)
        sums.append(jnp.sum(a.astype(F32) + b.astype(F32), axis=0, keepdims=True))
    bias = jnp.concatenate(sums, axis=1)

    def two_rows(v):
        hi = v.astype(BF).astype(F32)
        ids = lax.broadcasted_iota(jnp.int32, (TILE, feat), 0)
        return jnp.where(ids == 0, hi, jnp.where(ids == 1, v - hi, 0.0)).astype(BF)

    tail = two_rows(bias)
    for r in range(n_row):
        gpart[r, piece:piece + TILE, :] = tail
    g_cp = [send(gpart.at[(me_r + d) % n_row], grecv.at[d - 1], g_s.at[d - 1], g_r.at[d - 1], row_id(d))
            for d in range(1, n_row)]

    if cap == group:
        for k in range(cap):
            at = pos_ref[0, 0, k] % tbc
            alive = k < live_ref[0, 0]
            for j in range(tbc):
                lhs[k * blk:(k + 1) * blk, j * blk:(j + 1) * blk] = jnp.where(
                    alive & (at == j), blk_ref[0, 0, k], jnp.zeros((blk, blk), BF))

    for c in g_cp:
        c.wait_recv()
    acc = gpart[me_r].astype(F32)
    for d in range(1, n_row):
        acc += grecv[d - 1].astype(F32)
    tail = two_rows(jnp.sum(acc[piece:], axis=0, keepdims=True))
    if scatter:
        zsend[:, 0:part] = acc[:piece].astype(BF).reshape(n_z, part, feat)
        for q in range(n_z):
            zsend[q, part:] = tail
    else:
        zsend[0, 0:part] = acc[:piece].astype(BF)
        zsend[0, part:] = tail
    zpick = [zsend.at[(z + d) % n_z if scatter else 0] for d in range(n_z)]
    zz_cp = [send(zpick[d], zrecv.at[d - 1], z_s.at[d - 1], z_r.at[d - 1], z_id(d)) for d in range(1, n_z)]

    def forward(ch):
        out = []
        for d in range(1, n_z):
            z_cp[ch][d - 1].wait_recv()
            slot = gath[ch].at[((z + n_z - d) % n_z) * 2 + core]
            out.append(send(slot, slot, fw_s.at[ch, d - 1], fw_r.at[ch, d - 1], sib_id))
        return out

    def contribute(ch, fw):
        for c in fw:
            c.wait_recv()
        if cap == group:
            rhs = jnp.concatenate([gath[ch][pos_ref[0, 0, k] // tbc] for k in range(cap)], axis=0)
            cbuf[ch] = dot0(lhs[...], rhs).astype(BF).reshape(n_row, rows, fc)
        else:
            acc_ref = lhs
            acc_ref[...] = jnp.zeros_like(acc_ref)

            def turn(t, carry):
                for i in range(group):
                    k = t * group + i
                    p = pos_ref[0, 0, k]
                    rhs = gath[ch][p // tbc]
                    prod = dot0(blk_ref[0, 0, k], rhs)
                    alive = k < live_ref[0, 0]
                    for j in range(tbc):
                        acc_ref[j * blk:(j + 1) * blk] += jnp.where(alive & (p % tbc == j), prod, 0.0)
                return carry

            lax.fori_loop(0, cap // group, turn, 0)
            cbuf[ch] = acc_ref[...].astype(BF).reshape(n_row, rows, fc)
        return [send(cbuf.at[ch, (me_r + d) % n_row], rbuf.at[ch, d - 1], c_s.at[ch, d - 1], c_r.at[ch, d - 1], row_id(d))
                for d in range(1, n_row)]

    total = None

    def project(ch, cps):
        for c in cps:
            c.wait_recv()
        s = cbuf[ch, me_r].astype(F32)
        for d in range(1, n_row):
            s += rbuf[ch, d - 1].astype(F32)
        return lax.dot_general(s.astype(BF), w_ref[:, ch * fc:(ch + 1) * fc], (((1,), (1,)), ((), ())),
                               preferred_element_type=F32)

    base = core * half
    at_row = pl.ds(pl.multiple_of(base + me_r * piece, piece), piece)
    at_me = pl.ds(pl.multiple_of(base + me_r * piece + (z * part if scatter else 0), part), part)

    def z_sum():
        for c in zz_cp:
            c.wait_recv()
        acc = zpick[0][...].astype(F32)
        for d in range(1, n_z):
            acc += zrecv[d - 1].astype(F32)
        gb_ref[...] = jnp.sum(acc[part:], axis=0, keepdims=True)
        gw[at_me] = acc[:part].astype(BF)
        if not scatter:
            return []
        return [send(gw.at[at_me], gw.at[at_me], wz_s.at[d - 1], wz_r.at[d - 1], z_id(d)) for d in range(1, n_z)]

    fw = forward(0)
    wz_cp = z_sum()
    c_cp = [contribute(0, fw)]
    for c in wz_cp:
        c.wait_recv()
    wr_cp = [send(gw.at[at_row], gw.at[at_row], wr_s.at[d - 1], wr_r.at[d - 1], row_id(d)) for d in range(1, n_row)]
    wf_cp = [send(gw.at[at_row], gw.at[at_row], wf_s.at[0], wf_r.at[0], sib_id)]
    for ch in range(1, nch):
        fw = forward(ch)
        c_cp.append(contribute(ch, fw))
        more = project(ch - 1, c_cp[ch - 1])
        total = more if total is None else total + more
    for d in range(1, n_row):
        wr_cp[d - 1].wait_recv()
        src = pl.ds(pl.multiple_of(base + ((me_r + n_row - d) % n_row) * piece, piece), piece)
        wf_cp.append(send(gw.at[src], gw.at[src], wf_s.at[d], wf_r.at[d], sib_id))
    more = project(nch - 1, c_cp[nch - 1])
    total = more if total is None else total + more
    gi_ref[...] = total.astype(BF)
    for c in wf_cp:
        c.wait_recv()
    gw_ref[...] = gw[...]
    for c in sent:
        c.wait_send()


def body(n_row, n_col, grad_out, relu_mask, aggregated, weight, adj_blocks, block_pos, block_live):
    rows, feat = grad_out.shape
    cap, blk = adj_blocks.shape[2], adj_blocks.shape[-1]
    group = max(d for d in range(1, 17) if cap % d == 0)
    nch = 2
    fc = feat // nch
    n_z = n_col // 2
    piece = feat // 2 // n_row
    scatter = piece % (n_z * TILE) == 0
    part = piece // n_z if scatter else piece
    tbc = n_row * rows // blk
    if cap == group:
        lhs = pltpu.VMEM((cap * blk, tbc * blk), BF)
    else:
        lhs = pltpu.VMEM((tbc * blk, fc), F32)
    dma = pltpu.SemaphoreType.DMA
    scratch = [pltpu.VMEM((n_col, rows, fc), BF) for _ in range(nch)] + [
        lhs,
        pltpu.VMEM((nch, n_row, rows, fc), BF),
        pltpu.VMEM((nch, n_row - 1, rows, fc), BF),
        pltpu.VMEM((rows, feat // 2), BF),
        pltpu.VMEM((n_row, piece + TILE, feat), BF),
        pltpu.VMEM((n_row - 1, piece + TILE, feat), BF),
        pltpu.VMEM((n_z if scatter else 1, part + TILE, feat), BF),
        pltpu.VMEM((n_z - 1, part + TILE, feat), BF),
        pltpu.VMEM((feat, feat), BF),
    ]
    sems = [dma((nch, n_z)), dma((nch, n_z)), dma((nch, n_z - 1)), dma((nch, n_z - 1)),
            dma((nch, n_row - 1)), dma((nch, n_row - 1)), dma(()), dma(()),
            dma((n_row - 1,)), dma((n_row - 1,)), dma((n_z - 1,)), dma((n_z - 1,)),
            dma((n_z - 1,)), dma((n_z - 1,)), dma((n_row - 1,)), dma((n_row - 1,)),
            dma((n_row,)), dma((n_row,))]
    vm = pl.BlockSpec(memory_space=pltpu.VMEM)
    sm = pl.BlockSpec(memory_space=pltpu.SMEM)
    gi, gw, gb = pl.pallas_call(
        functools.partial(kernel, (n_row, n_col, nch, cap, group, scatter)),
        out_shape=(jax.ShapeDtypeStruct((rows, feat), BF),
                   jax.ShapeDtypeStruct((feat, feat), BF),
                   jax.ShapeDtypeStruct((1, feat), F32)),
        in_specs=[vm, vm, vm, vm, vm, sm, sm],
        out_specs=(vm, vm, vm),
        scratch_shapes=scratch + sems,
        compiler_params=pltpu.CompilerParams(collective_id=0, has_side_effects=True,
                                             vmem_limit_bytes=48 * 1024 * 1024),
    )(grad_out, relu_mask, aggregated, weight, adj_blocks, block_pos, block_live)
    factor = 1.0 / math.sqrt(rows * n_row * n_col)
    return gi.reshape(1, rows, feat), gw.astype(F32) * factor, gb.reshape(feat) * factor


def solution(mesh):
    return jax.shard_map(
        functools.partial(body, mesh.shape["row"], mesh.shape["col"]),
        mesh=mesh,
        in_specs=(
            P(("row", "col"), None),
            P(("row", "col"), None),
            P(("row", "col"), None),
            P(),
            P("row", "col", None, None, None),
            P("row", "col", None),
            P("row", "col"),
        ),
        out_specs=(P("col", "row", None), P(), P()),
        check_vma=False,
    )
```

```python
import functools
import math

import jax
import jax.numpy as jnp
from jax import lax
from jax.experimental import pallas as pl
from jax.experimental.pallas import tpu as pltpu
from jax.sharding import PartitionSpec as P

MESH = pl.DeviceIdType.MESH
BF = jnp.bfloat16
F32 = jnp.float32
TILE = 16


def dot0(a, b):
    return lax.dot_general(a, b, (((0,), (0,)), ((), ())), preferred_element_type=F32)


def kernel(cfg, go_ref, mask_ref, agg_ref, w_ref, blk_ref, pos_ref, live_ref,
           gi_ref, gw_ref, gb_ref, *scr):
    n_row, n_col, nch, cap, group, scatter = cfg
    n_z = n_col // 2
    gath = scr[:nch]
    lhs, cbuf, rbuf, asib, gpart, grecv, zsend, zrecv, gw, go_v, mask_v, agg_v, w_v, blk_v, bsend, brecv = scr[nch:nch + 16]
    (ag_s, ag_r, fw_s, fw_r, c_s, c_r, as_s, as_r, g_s, g_r, z_s, z_r, wz_s, wz_r, wr_s, wr_r, wf_s, wf_r,
     b_s, b_r, in_s) = scr[nch + 16:]
    rows, feat = go_ref.shape
    fc = feat // nch
    blk = blk_ref.shape[-1]
    tbc = n_row * rows // blk
    half = feat // 2
    piece = half // n_row
    part = piece // n_z if scatter else piece
    me_r, me_c = lax.axis_index("row"), lax.axis_index("col")
    z, core = me_c // 2, me_c % 2
    sib = z * 2 + 1 - core
    sib_id = (me_r, sib)

    def row_id(d):
        return ((me_r + d) % n_row, me_c)

    def z_id(d):
        return (me_r, ((z + d) % n_z) * 2 + core)

    other = pl.ds(pl.multiple_of((1 - core) * half, half), half)
    mine = pl.ds(pl.multiple_of(core * half, half), half)
    loads = [pltpu.make_async_copy(src, dst, in_s.at[i]) for i, (src, dst) in enumerate((
        (go_ref, go_v), (mask_ref, mask_v), (agg_ref.at[:, mine], agg_v), (blk_ref.at[0, 0], blk_v), (w_ref, w_v)))]
    for c in loads:
        c.start()

    sent = []

    def send(src, dst, s, r, dev):
        c = pltpu.make_async_remote_copy(src_ref=src, dst_ref=dst, send_sem=s, recv_sem=r,
                                         device_id=dev, device_id_type=MESH)
        c.start()
        sent.append(c)
        return c

    barrier = pltpu.get_barrier_semaphore()
    peers = [sib_id] + [z_id(d) for d in range(1, n_z)] + [row_id(d) for d in range(1, n_row)]
    for p in peers:
        pl.semaphore_signal(barrier, inc=1, device_id=p, device_id_type=MESH)

    loads[0].wait()
    loads[1].wait()
    for ch in range(nch):
        cols = slice(ch * fc, (ch + 1) * fc)
        gath[ch][me_c] = go_v[:, cols] * mask_v[:, cols].astype(F32).astype(BF)

    pl.semaphore_wait(barrier, len(peers))

    sib_cp, z_cp = [], []
    agg_cp = send(agg_ref.at[:, other], asib, as_s, as_r, sib_id)
    for ch in range(nch):
        own = gath[ch].at[me_c]
        sib_cp.append(send(own, own, ag_s.at[ch, 0], ag_r.at[ch, 0], sib_id))
        z_cp.append([send(own, own, ag_s.at[ch, d], ag_r.at[ch, d], z_id(d)) for d in range(1, n_z)])

    loads[2].wait()
    agg_cp.wait_recv()
    for ch in range(nch):
        cols = slice(ch * fc, (ch + 1) * fc)
        sib_cp[ch].wait_recv()
        g = dot0(agg_v[...], gath[ch][me_c]) + dot0(asib[...], gath[ch][sib])
        gpart[:, :, cols] = g.astype(BF).reshape(n_row, piece, fc)
    g_cp = [send(gpart.at[(me_r + d) % n_row], grecv.at[d - 1], g_s.at[d - 1], g_r.at[d - 1], row_id(d))
            for d in range(1, n_row)]

    loads[3].wait()
    if cap == group:
        for k in range(cap):
            at = pos_ref[0, 0, k] % tbc
            alive = k < live_ref[0, 0]
            for j in range(tbc):
                lhs[k * blk:(k + 1) * blk, j * blk:(j + 1) * blk] = jnp.where(
                    alive & (at == j), blk_v[k], jnp.zeros((blk, blk), BF))

    for c in g_cp:
        c.wait_recv()
    acc = gpart[me_r].astype(F32)
    for d in range(1, n_row):
        acc += grecv[d - 1].astype(F32)
    zsend[...] = acc.astype(BF).reshape(zsend.shape)
    zpick = [zsend.at[(z + d) % n_z if scatter else 0] for d in range(n_z)]
    zz_cp = [send(zpick[d], zrecv.at[d - 1], z_s.at[d - 1], z_r.at[d - 1], z_id(d)) for d in range(1, n_z)]

    def forward(ch):
        out = []
        for d in range(1, n_z):
            z_cp[ch][d - 1].wait_recv()
            slot = gath[ch].at[((z + n_z - d) % n_z) * 2 + core]
            out.append(send(slot, slot, fw_s.at[ch, d - 1], fw_r.at[ch, d - 1], sib_id))
        return out

    def contribute(ch, fw):
        for c in fw:
            c.wait_recv()
        if cap == group:
            rhs = jnp.concatenate([gath[ch][pos_ref[0, 0, k] // tbc] for k in range(cap)], axis=0)
            cbuf[ch] = dot0(lhs[...], rhs).astype(BF).reshape(n_row, rows, fc)
        else:
            acc_ref = lhs
            acc_ref[...] = jnp.zeros_like(acc_ref)

            def turn(t, carry):
                for i in range(group):
                    k = t * group + i
                    p = pos_ref[0, 0, k]
                    rhs = gath[ch][p // tbc]
                    prod = dot0(blk_v[k], rhs)
                    alive = k < live_ref[0, 0]
                    for j in range(tbc):
                        acc_ref[j * blk:(j + 1) * blk] += jnp.where(alive & (p % tbc == j), prod, 0.0)
                return carry

            lax.fori_loop(0, cap // group, turn, 0)
            cbuf[ch] = acc_ref[...].astype(BF).reshape(n_row, rows, fc)
        return [send(cbuf.at[ch, (me_r + d) % n_row], rbuf.at[ch, d - 1], c_s.at[ch, d - 1], c_r.at[ch, d - 1], row_id(d))
                for d in range(1, n_row)]

    total = None

    def project(ch, cps):
        for c in cps:
            c.wait_recv()
        s = cbuf[ch, me_r].astype(F32)
        for d in range(1, n_row):
            s += rbuf[ch, d - 1].astype(F32)
        return lax.dot_general(s.astype(BF), w_v[:, ch * fc:(ch + 1) * fc], (((1,), (1,)), ((), ())),
                               preferred_element_type=F32)

    base = core * half
    at_row = pl.ds(pl.multiple_of(base + me_r * piece, piece), piece)
    at_me = pl.ds(pl.multiple_of(base + me_r * piece + (z * part if scatter else 0), part), part)

    def z_sum():
        for c in zz_cp:
            c.wait_recv()
        acc = zpick[0][...].astype(F32)
        for d in range(1, n_z):
            acc += zrecv[d - 1].astype(F32)
        gw[at_me] = acc.astype(BF)
        if not scatter:
            return []
        return [send(gw.at[at_me], gw.at[at_me], wz_s.at[d - 1], wz_r.at[d - 1], z_id(d)) for d in range(1, n_z)]

    lanes = 128
    c_cp = [contribute(0, forward(0))]
    wz_cp = z_sum()
    for ch in range(1, nch):
        c_cp.append(contribute(ch, forward(ch)))
    for c in wz_cp:
        c.wait_recv()
    wr_cp = [send(gw.at[at_row], gw.at[at_row], wr_s.at[d - 1], wr_r.at[d - 1], row_id(d)) for d in range(1, n_row)]
    wf_cp = [send(gw.at[at_row], gw.at[at_row], wf_s.at[0], wf_r.at[0], sib_id)]

    bsend[...] = jnp.zeros_like(bsend)
    ones = jnp.ones((TILE, n_col * rows), BF)
    for ch in range(nch):
        sums = lax.dot_general(ones, gath[ch][...].reshape(n_col * rows, fc), (((1,), (0,)), ((), ())),
                               preferred_element_type=F32)
        for i in range(fc // lanes):
            at = ch * (fc // lanes) + i
            bsend[at:at + 1, :] = sums[0:1, i * lanes:(i + 1) * lanes]
    b_cp = [send(bsend, brecv.at[d - 1], b_s.at[d - 1], b_r.at[d - 1], row_id(d)) for d in range(1, n_row)]

    loads[4].wait()
    for ch in range(nch - 1):
        more = project(ch, c_cp[ch])
        total = more if total is None else total + more
    for d in range(1, n_row):
        wr_cp[d - 1].wait_recv()
        src = pl.ds(pl.multiple_of(base + ((me_r + n_row - d) % n_row) * piece, piece), piece)
        wf_cp.append(send(gw.at[src], gw.at[src], wf_s.at[d], wf_r.at[d], sib_id))
    more = project(nch - 1, c_cp[nch - 1])
    total = more if total is None else total + more
    gi_ref[...] = total.astype(BF)
    bias = bsend[...]
    for d in range(1, n_row):
        b_cp[d - 1].wait_recv()
        bias += brecv[d - 1]
    gb_ref[...] = bias
    for c in wf_cp:
        c.wait_recv()
    gw_ref[...] = gw[...]
    for c in sent:
        c.wait_send()


def body(n_row, n_col, grad_out, relu_mask, aggregated, weight, adj_blocks, block_pos, block_live):
    rows, feat = grad_out.shape
    cap, blk = adj_blocks.shape[2], adj_blocks.shape[-1]
    group = max(d for d in range(1, 17) if cap % d == 0)
    nch = 2
    fc = feat // nch
    n_z = n_col // 2
    piece = feat // 2 // n_row
    scatter = piece % (n_z * TILE) == 0
    part = piece // n_z if scatter else piece
    tbc = n_row * rows // blk
    brows = -(-feat // 1024) * 8
    if cap == group:
        lhs = pltpu.VMEM((cap * blk, tbc * blk), BF)
    else:
        lhs = pltpu.VMEM((tbc * blk, fc), F32)
    dma = pltpu.SemaphoreType.DMA
    scratch = [pltpu.VMEM((n_col, rows, fc), BF) for _ in range(nch)] + [
        lhs,
        pltpu.VMEM((nch, n_row, rows, fc), BF),
        pltpu.VMEM((nch, n_row - 1, rows, fc), BF),
        pltpu.VMEM((rows, feat // 2), BF),
        pltpu.VMEM((n_row, piece, feat), BF),
        pltpu.VMEM((n_row - 1, piece, feat), BF),
        pltpu.VMEM((n_z if scatter else 1, part, feat), BF),
        pltpu.VMEM((n_z - 1, part, feat), BF),
        pltpu.VMEM((feat, feat), BF),
        pltpu.VMEM((rows, feat), BF),
        pltpu.VMEM((rows, feat), jnp.int32),
        pltpu.VMEM((rows, feat // 2), BF),
        pltpu.VMEM((feat, feat), BF),
        pltpu.VMEM((cap, blk, blk), BF),
        pltpu.VMEM((brows, 128), F32),
        pltpu.VMEM((n_row - 1, brows, 128), F32),
    ]
    sems = [dma((nch, n_z)), dma((nch, n_z)), dma((nch, n_z - 1)), dma((nch, n_z - 1)),
            dma((nch, n_row - 1)), dma((nch, n_row - 1)), dma(()), dma(()),
            dma((n_row - 1,)), dma((n_row - 1,)), dma((n_z - 1,)), dma((n_z - 1,)),
            dma((n_z - 1,)), dma((n_z - 1,)), dma((n_row - 1,)), dma((n_row - 1,)),
            dma((n_row,)), dma((n_row,)), dma((n_row - 1,)), dma((n_row - 1,)), dma((5,))]
    vm = pl.BlockSpec(memory_space=pltpu.VMEM)
    hbm = pl.BlockSpec(memory_space=pl.ANY)
    sm = pl.BlockSpec(memory_space=pltpu.SMEM)
    gi, gw, gb = pl.pallas_call(
        functools.partial(kernel, (n_row, n_col, nch, cap, group, scatter)),
        out_shape=(jax.ShapeDtypeStruct((rows, feat), BF),
                   jax.ShapeDtypeStruct((feat, feat), BF),
                   jax.ShapeDtypeStruct((brows, 128), F32)),
        in_specs=[hbm, hbm, hbm, hbm, hbm, sm, sm],
        out_specs=(vm, vm, vm),
        scratch_shapes=scratch + sems,
        compiler_params=pltpu.CompilerParams(collective_id=0, has_side_effects=True,
                                             vmem_limit_bytes=56 * 1024 * 1024),
    )(grad_out, relu_mask, aggregated, weight, adj_blocks, block_pos, block_live)
    factor = 1.0 / math.sqrt(rows * n_row * n_col)
    return gi.reshape(1, rows, feat), gw.astype(F32) * factor, gb.reshape(-1)[:feat] * factor


def solution(mesh):
    return jax.shard_map(
        functools.partial(body, mesh.shape["row"], mesh.shape["col"]),
        mesh=mesh,
        in_specs=(
            P(("row", "col"), None),
            P(("row", "col"), None),
            P(("row", "col"), None),
            P(),
            P("row", "col", None, None, None),
            P("row", "col", None),
            P("row", "col"),
        ),
        out_specs=(P("col", "row", None), P(), P()),
        check_vma=False,
    )
```

```python
import functools
import math

import jax
import jax.numpy as jnp
from jax import lax
from jax.experimental import pallas as pl
from jax.experimental.pallas import tpu as pltpu
from jax.sharding import PartitionSpec as P

MESH = pl.DeviceIdType.MESH
BF = jnp.bfloat16
F32 = jnp.float32
TILE = 16


def dot0(a, b):
    return lax.dot_general(a, b, (((0,), (0,)), ((), ())), preferred_element_type=F32)


def kernel(cfg, go_ref, mask_ref, agg_ref, w_ref, blk_ref, pos_ref, live_ref,
           gi_ref, gw_ref, gb_ref, *scr):
    n_row, n_col, nch, cap, group, scatter = cfg
    n_z = n_col // 2
    gath = scr[:nch]
    lhs, cbuf, rbuf, asib, gpart, grecv, zsend, zrecv, gw, go_v, mask_v, agg_v, w_v, blk_v, bsend, brecv, gi_v = scr[nch:nch + 17]
    (ag_s, ag_r, fw_s, fw_r, c_s, c_r, as_s, as_r, g_s, g_r, z_s, z_r, wz_s, wz_r, wr_s, wr_r, wf_s, wf_r,
     b_s, b_r, in_s, sb_s, sb_r, out_s) = scr[nch + 17:]
    rows, feat = go_ref.shape
    fc = feat // nch
    blk = blk_ref.shape[-1]
    tbc = n_row * rows // blk
    half = feat // 2
    piece = half // n_row
    part = piece // n_z if scatter else piece
    me_r, me_c = lax.axis_index("row"), lax.axis_index("col")
    z, core = me_c // 2, me_c % 2
    sib = z * 2 + 1 - core
    sib_id = (me_r, sib)

    def row_id(d):
        return ((me_r + d) % n_row, me_c)

    def z_id(d):
        return (me_r, ((z + d) % n_z) * 2 + core)

    other = pl.ds(pl.multiple_of((1 - core) * half, half), half)
    mine = pl.ds(pl.multiple_of(core * half, half), half)
    loads = [pltpu.make_async_copy(src, dst, in_s.at[i]) for i, (src, dst) in enumerate((
        (go_ref, go_v), (mask_ref, mask_v), (agg_ref.at[:, mine], agg_v), (blk_ref.at[0, 0], blk_v), (w_ref, w_v)))]
    for c in loads:
        c.start()

    sent = []

    def copy(src, dst, s, r, dev):
        return pltpu.make_async_remote_copy(src_ref=src, dst_ref=dst, send_sem=s, recv_sem=r,
                                               device_id=dev, device_id_type=MESH)

    def send(*what):
        c = copy(*what)
        c.start()
        sent.append((None, lambda: copy(*what)))
        return c

    def send_when(now, make):
        pl.when(now)(lambda: make().start())
        sent.append((now, make))

    barrier = pltpu.get_barrier_semaphore()
    peers = [sib_id] + [z_id(d) for d in range(1, n_z)] + [row_id(d) for d in range(1, n_row)]
    for p in peers:
        pl.semaphore_signal(barrier, inc=1, device_id=p, device_id_type=MESH)

    loads[0].wait()
    loads[1].wait()
    for ch in range(nch):
        cols = slice(ch * fc, (ch + 1) * fc)
        gath[ch][me_c] = go_v[:, cols] * mask_v[:, cols].astype(F32).astype(BF)

    pl.semaphore_wait(barrier, len(peers))

    has_next = (z < n_z - 1, z > 0)
    next_id = ((me_r, me_c + 2), (me_r, me_c - 2))
    sib_cp = []
    agg_cp = send(agg_ref.at[:, other], asib, as_s, as_r, sib_id)
    for ch in range(nch):
        own = gath[ch].at[me_c]
        sib_cp.append(send(own, own, sb_s.at[ch], sb_r.at[ch], sib_id))
        for way in range(2):
            send_when(has_next[way], lambda ch=ch, way=way, own=own: copy(
                own, own, ag_s.at[ch, way, 0], ag_r.at[ch, way, 0], next_id[way]))

    loads[2].wait()
    agg_cp.wait_recv()
    for ch in range(nch):
        cols = slice(ch * fc, (ch + 1) * fc)
        sib_cp[ch].wait_recv()
        g = dot0(agg_v[...], gath[ch][me_c]) + dot0(asib[...], gath[ch][sib])
        gpart[:, :, cols] = g.astype(BF).reshape(n_row, piece, fc)
    g_cp = [send(gpart.at[(me_r + d) % n_row], grecv.at[d - 1], g_s.at[d - 1], g_r.at[d - 1], row_id(d))
            for d in range(1, n_row)]

    loads[3].wait()
    if cap == group:
        for k in range(cap):
            at = pos_ref[0, 0, k] % tbc
            alive = k < live_ref[0, 0]
            for j in range(tbc):
                lhs[k * blk:(k + 1) * blk, j * blk:(j + 1) * blk] = jnp.where(
                    alive & (at == j), blk_v[k], jnp.zeros((blk, blk), BF))

    def arrival(way, step):
        src = z - 1 - step if way == 0 else z + 1 + step
        return src, (src >= 0 if way == 0 else src <= n_z - 1)

    def relay(ch, step):
        for way in range(2):
            src, there = arrival(way, step)

            slot = gath[ch].at[src * 2 + core]
            on = there & has_next[way]

            def hop(step, way=way, slot=slot):
                return copy(slot, slot, ag_s.at[ch, way, step], ag_r.at[ch, way, step], next_id[way])

            def over(way=way, slot=slot):
                return copy(slot, slot, fw_s.at[ch, way, step], fw_r.at[ch, way, step], sib_id)

            pl.when(there)(lambda hop=hop: hop(step).wait_recv())
            if step + 1 < n_z - 1:
                send_when(on, functools.partial(hop, step + 1))
            send_when(there, over)

    def gathered(ch):
        for step in range(n_z - 1):
            for way in range(2):
                src, there = arrival(way, step)

                def come(way=way, step=step, src=src):
                    slot = gath[ch].at[src * 2 + 1 - core]
                    copy(slot, slot, fw_s.at[ch, way, step], fw_r.at[ch, way, step], sib_id).wait_recv()

                pl.when(there)(come)

    def contribute(ch):
        gathered(ch)
        if cap == group:
            rhs = jnp.concatenate([gath[ch][pos_ref[0, 0, k] // tbc] for k in range(cap)], axis=0)
            cbuf[ch] = dot0(lhs[...], rhs).astype(BF).reshape(n_row, rows, fc)
        else:
            acc_ref = lhs
            acc_ref[...] = jnp.zeros_like(acc_ref)

            def turn(t, carry):
                for i in range(group):
                    k = t * group + i
                    p = pos_ref[0, 0, k]
                    rhs = gath[ch][p // tbc]
                    prod = dot0(blk_v[k], rhs)
                    alive = k < live_ref[0, 0]
                    for j in range(tbc):
                        acc_ref[j * blk:(j + 1) * blk] += jnp.where(alive & (p % tbc == j), prod, 0.0)
                return carry

            lax.fori_loop(0, cap // group, turn, 0)
            cbuf[ch] = acc_ref[...].astype(BF).reshape(n_row, rows, fc)
        return [send(cbuf.at[ch, (me_r + d) % n_row], rbuf.at[ch, d - 1], c_s.at[ch, d - 1], c_r.at[ch, d - 1], row_id(d))
                for d in range(1, n_row)]

    total = None

    def project(ch, cps):
        for c in cps:
            c.wait_recv()
        s = cbuf[ch, me_r].astype(F32)
        for d in range(1, n_row):
            s += rbuf[ch, d - 1].astype(F32)
        return lax.dot_general(s.astype(BF), w_v[:, ch * fc:(ch + 1) * fc], (((1,), (1,)), ((), ())),
                               preferred_element_type=F32)

    base = core * half
    at_row = pl.ds(pl.multiple_of(base + me_r * piece, piece), piece)
    at_me = pl.ds(pl.multiple_of(base + me_r * piece + (z * part if scatter else 0), part), part)

    for ch in range(nch):
        relay(ch, 0)
    for c in g_cp:
        c.wait_recv()
    acc = gpart[me_r].astype(F32)
    for d in range(1, n_row):
        acc += grecv[d - 1].astype(F32)
    zsend[...] = acc.astype(BF).reshape(zsend.shape)
    zpick = [zsend.at[(z + d) % n_z if scatter else 0] for d in range(n_z)]
    zz_cp = [send(zpick[d], zrecv.at[d - 1], z_s.at[d - 1], z_r.at[d - 1], z_id(d)) for d in range(1, n_z)]

    def z_sum():
        for c in zz_cp:
            c.wait_recv()
        acc = zpick[0][...].astype(F32)
        for d in range(1, n_z):
            acc += zrecv[d - 1].astype(F32)
        gw[at_me] = acc.astype(BF)
        if not scatter:
            return []
        return [send(gw.at[at_me], gw.at[at_me], wz_s.at[d - 1], wz_r.at[d - 1], z_id(d)) for d in range(1, n_z)]

    lanes = 128
    for step in range(1, n_z - 1):
        for ch in range(nch):
            relay(ch, step)
            if step == n_z - 2 and ch == 0:
                c_cp = [contribute(0)]
                wz_cp = z_sum()
    for ch in range(1, nch):
        c_cp.append(contribute(ch))
    for c in wz_cp:
        c.wait_recv()
    wr_cp = [send(gw.at[at_row], gw.at[at_row], wr_s.at[d - 1], wr_r.at[d - 1], row_id(d)) for d in range(1, n_row)]
    wf_cp = [send(gw.at[at_row], gw.at[at_row], wf_s.at[0], wf_r.at[0], sib_id)]

    bsend[...] = jnp.zeros_like(bsend)
    ones = jnp.ones((TILE, n_col * rows), BF)
    for ch in range(nch):
        sums = lax.dot_general(ones, gath[ch][...].reshape(n_col * rows, fc), (((1,), (0,)), ((), ())),
                               preferred_element_type=F32)
        for i in range(fc // lanes):
            at = ch * (fc // lanes) + i
            bsend[at:at + 1, :] = sums[0:1, i * lanes:(i + 1) * lanes]
    b_cp = [send(bsend, brecv.at[d - 1], b_s.at[d - 1], b_r.at[d - 1], row_id(d)) for d in range(1, n_row)]

    loads[4].wait()
    for ch in range(nch - 1):
        more = project(ch, c_cp[ch])
        total = more if total is None else total + more
    for d in range(1, n_row):
        wr_cp[d - 1].wait_recv()
        src = pl.ds(pl.multiple_of(base + ((me_r + n_row - d) % n_row) * piece, piece), piece)
        wf_cp.append(send(gw.at[src], gw.at[src], wf_s.at[d], wf_r.at[d], sib_id))
    outs = [pltpu.make_async_copy(gw.at[mine], gw_ref.at[mine], out_s.at[0])]
    outs[0].start()
    more = project(nch - 1, c_cp[nch - 1])
    total = more if total is None else total + more
    gi_v[...] = total.astype(BF)
    outs.append(pltpu.make_async_copy(gi_v, gi_ref, out_s.at[1]))
    outs[-1].start()
    bias = bsend[...]
    for d in range(1, n_row):
        b_cp[d - 1].wait_recv()
        bias += brecv[d - 1]
    gb_ref[...] = bias
    for c in wf_cp:
        c.wait_recv()
    outs.append(pltpu.make_async_copy(gw.at[other], gw_ref.at[other], out_s.at[2]))
    outs[-1].start()
    for now, make in sent:
        if now is None:
            make().wait_send()
        else:
            pl.when(now)(lambda make=make: make().wait_send())
    for c in outs:
        c.wait()


def finish(factor, gi_ref, gw_ref, gb_ref, gi_out, gw_out, gb_out, w_in, w_out, b_in, b_out, i_s, o_s):
    n = w_in.shape[0]
    step = w_in.shape[1]
    ins = [pltpu.make_async_copy(gw_ref.at[i * step:(i + 1) * step], w_in.at[i], i_s.at[i]) for i in range(n)]
    ins.append(pltpu.make_async_copy(gb_ref, b_in, i_s.at[n]))
    outs = [pltpu.make_async_copy(w_out.at[i], gw_out.at[i * step:(i + 1) * step], o_s.at[i]) for i in range(n)]
    outs.append(pltpu.make_async_copy(b_out, gb_out, o_s.at[n]))
    outs.append(pltpu.make_async_copy(gi_ref, gi_out.at[0], o_s.at[n + 1]))
    for c in ins:
        c.start()
    outs[n + 1].start()
    for i in range(n):
        ins[i].wait()
        w_out[i] = w_in[i].astype(F32) * factor
        outs[i].start()
    ins[n].wait()
    for i in range(b_out.shape[1] // 128):
        b_out[:, i * 128:(i + 1) * 128] = b_in[i:i + 1, :] * factor
    outs[n].start()
    for c in outs:
        c.wait()


def body(n_row, n_col, grad_out, relu_mask, aggregated, weight, adj_blocks, block_pos, block_live):
    rows, feat = grad_out.shape
    cap, blk = adj_blocks.shape[2], adj_blocks.shape[-1]
    group = max(d for d in range(1, 17) if cap % d == 0)
    nch = 2
    fc = feat // nch
    n_z = n_col // 2
    piece = feat // 2 // n_row
    scatter = piece % (n_z * TILE) == 0
    part = piece // n_z if scatter else piece
    tbc = n_row * rows // blk
    brows = -(-feat // 1024) * 8
    if cap == group:
        lhs = pltpu.VMEM((cap * blk, tbc * blk), BF)
    else:
        lhs = pltpu.VMEM((tbc * blk, fc), F32)
    dma = pltpu.SemaphoreType.DMA
    scratch = [pltpu.VMEM((n_col, rows, fc), BF) for _ in range(nch)] + [
        lhs,
        pltpu.VMEM((nch, n_row, rows, fc), BF),
        pltpu.VMEM((nch, n_row - 1, rows, fc), BF),
        pltpu.VMEM((rows, feat // 2), BF),
        pltpu.VMEM((n_row, piece, feat), BF),
        pltpu.VMEM((n_row - 1, piece, feat), BF),
        pltpu.VMEM((n_z if scatter else 1, part, feat), BF),
        pltpu.VMEM((n_z - 1, part, feat), BF),
        pltpu.VMEM((feat, feat), BF),
        pltpu.VMEM((rows, feat), BF),
        pltpu.VMEM((rows, feat), jnp.int32),
        pltpu.VMEM((rows, feat // 2), BF),
        pltpu.VMEM((feat, feat), BF),
        pltpu.VMEM((cap, blk, blk), BF),
        pltpu.VMEM((brows, 128), F32),
        pltpu.VMEM((n_row - 1, brows, 128), F32),
        pltpu.VMEM((rows, feat), BF),
    ]
    sems = [dma((nch, 2, n_z - 1)), dma((nch, 2, n_z - 1)), dma((nch, 2, n_z - 1)), dma((nch, 2, n_z - 1)),
            dma((nch, n_row - 1)), dma((nch, n_row - 1)), dma(()), dma(()),
            dma((n_row - 1,)), dma((n_row - 1,)), dma((n_z - 1,)), dma((n_z - 1,)),
            dma((n_z - 1,)), dma((n_z - 1,)), dma((n_row - 1,)), dma((n_row - 1,)),
            dma((n_row,)), dma((n_row,)), dma((n_row - 1,)), dma((n_row - 1,)), dma((5,)),
            dma((nch,)), dma((nch,)), dma((3,))]
    vm = pl.BlockSpec(memory_space=pltpu.VMEM)
    hbm = pl.BlockSpec(memory_space=pl.ANY)
    sm = pl.BlockSpec(memory_space=pltpu.SMEM)
    gi, gw, gb = pl.pallas_call(
        functools.partial(kernel, (n_row, n_col, nch, cap, group, scatter)),
        out_shape=(jax.ShapeDtypeStruct((rows, feat), BF),
                   jax.ShapeDtypeStruct((feat, feat), BF),
                   jax.ShapeDtypeStruct((brows, 128), F32)),
        in_specs=[hbm, hbm, hbm, hbm, hbm, sm, sm],
        out_specs=(hbm, hbm, vm),
        scratch_shapes=scratch + sems,
        compiler_params=pltpu.CompilerParams(collective_id=0, has_side_effects=True,
                                             vmem_limit_bytes=56 * 1024 * 1024),
    )(grad_out, relu_mask, aggregated, weight, adj_blocks, block_pos, block_live)
    factor = 1.0 / math.sqrt(rows * n_row * n_col)
    gi, gw, gb = pl.pallas_call(
        functools.partial(finish, factor),
        out_shape=(jax.ShapeDtypeStruct((1, rows, feat), BF),
                   jax.ShapeDtypeStruct((feat, feat), F32),
                   jax.ShapeDtypeStruct((1, feat), F32)),
        in_specs=[hbm, hbm, hbm],
        out_specs=(hbm, hbm, hbm),
        scratch_shapes=[pltpu.VMEM((2, feat // 2, feat), BF), pltpu.VMEM((2, feat // 2, feat), F32),
                        pltpu.VMEM((brows, 128), F32), pltpu.VMEM((1, feat), F32), dma((3,)), dma((4,))],
        compiler_params=pltpu.CompilerParams(vmem_limit_bytes=56 * 1024 * 1024),
    )(gi, gw, gb)
    return gi, gw, gb.reshape(feat)


def solution(mesh):
    return jax.shard_map(
        functools.partial(body, mesh.shape["row"], mesh.shape["col"]),
        mesh=mesh,
        in_specs=(
            P(("row", "col"), None),
            P(("row", "col"), None),
            P(("row", "col"), None),
            P(),
            P("row", "col", None, None, None),
            P("row", "col", None),
            P("row", "col"),
        ),
        out_specs=(P("col", "row", None), P(), P()),
        check_vma=False,
    )
```

```python
import functools
import math

import jax
import jax.numpy as jnp
from jax import lax
from jax.experimental import pallas as pl
from jax.experimental.pallas import tpu as pltpu
from jax.sharding import PartitionSpec as P

MESH = pl.DeviceIdType.MESH
BF = jnp.bfloat16
F32 = jnp.float32
TILE = 16


def dot0(a, b):
    return lax.dot_general(a, b, (((0,), (0,)), ((), ())), preferred_element_type=F32)


def kernel(cfg, go_ref, mask_ref, agg_ref, w_ref, blk_ref, pos_ref, live_ref,
           gi_ref, gw_ref, gb_ref, *scr):
    n_row, n_col, nch, cap, group, scatter = cfg
    n_z = n_col // 2
    gath = scr[:nch]
    lhs, cbuf, rbuf, asib, gpart, grecv, zsend, zrecv, gw, go_v, mask_v, agg_v, w_v, blk_v, bsend, brecv = scr[nch:nch + 16]
    (ag_s, ag_r, fw_s, fw_r, c_s, c_r, as_s, as_r, g_s, g_r, z_s, z_r, wz_s, wz_r, wr_s, wr_r, wf_s, wf_r,
     b_s, b_r, in_s, sb_s, sb_r) = scr[nch + 16:]
    rows, feat = go_ref.shape
    fc = feat // nch
    blk = blk_ref.shape[-1]
    tbc = n_row * rows // blk
    half = feat // 2
    piece = half // n_row
    part = piece // n_z if scatter else piece
    me_r, me_c = lax.axis_index("row"), lax.axis_index("col")
    z, core = me_c // 2, me_c % 2
    sib = z * 2 + 1 - core
    sib_id = (me_r, sib)

    def row_id(d):
        return ((me_r + d) % n_row, me_c)

    def z_id(d):
        return (me_r, ((z + d) % n_z) * 2 + core)

    other = pl.ds(pl.multiple_of((1 - core) * half, half), half)
    mine = pl.ds(pl.multiple_of(core * half, half), half)
    loads = [pltpu.make_async_copy(src, dst, in_s.at[i]) for i, (src, dst) in enumerate((
        (go_ref, go_v), (mask_ref, mask_v), (agg_ref.at[:, mine], agg_v), (blk_ref.at[0, 0], blk_v), (w_ref, w_v)))]
    for c in loads:
        c.start()

    sent = []

    def copy(src, dst, s, r, dev):
        return pltpu.make_async_remote_copy(src_ref=src, dst_ref=dst, send_sem=s, recv_sem=r,
                                               device_id=dev, device_id_type=MESH)

    def send(*what):
        c = copy(*what)
        c.start()
        sent.append((None, lambda: copy(*what)))
        return c

    def send_when(now, make):
        pl.when(now)(lambda: make().start())
        sent.append((now, make))

    barrier = pltpu.get_barrier_semaphore()
    peers = [sib_id] + [z_id(d) for d in range(1, n_z)] + [row_id(d) for d in range(1, n_row)]
    for p in peers:
        pl.semaphore_signal(barrier, inc=1, device_id=p, device_id_type=MESH)

    loads[0].wait()
    loads[1].wait()
    for ch in range(nch):
        cols = slice(ch * fc, (ch + 1) * fc)
        gath[ch][me_c] = go_v[:, cols] * mask_v[:, cols].astype(F32).astype(BF)

    pl.semaphore_wait(barrier, len(peers))

    has_next = (z < n_z - 1, z > 0)
    next_id = ((me_r, me_c + 2), (me_r, me_c - 2))
    sib_cp = []
    agg_cp = send(agg_ref.at[:, other], asib, as_s, as_r, sib_id)
    for ch in range(nch):
        own = gath[ch].at[me_c]
        sib_cp.append(send(own, own, sb_s.at[ch], sb_r.at[ch], sib_id))

    def depart(ch):
        own = gath[ch].at[me_c]
        for way in range(2):
            send_when(has_next[way], lambda way=way: copy(
                own, own, ag_s.at[ch, way, 0], ag_r.at[ch, way, 0], next_id[way]))

    depart(0)

    loads[2].wait()
    agg_cp.wait_recv()
    for ch in range(nch):
        cols = slice(ch * fc, (ch + 1) * fc)
        sib_cp[ch].wait_recv()
        g = dot0(agg_v[...], gath[ch][me_c]) + dot0(asib[...], gath[ch][sib])
        gpart[:, :, cols] = g.astype(BF).reshape(n_row, piece, fc)
    g_cp = [send(gpart.at[(me_r + d) % n_row], grecv.at[d - 1], g_s.at[d - 1], g_r.at[d - 1], row_id(d))
            for d in range(1, n_row)]

    def arrival(way, step):
        src = z - 1 - step if way == 0 else z + 1 + step
        return src, (src >= 0 if way == 0 else src <= n_z - 1)

    def relay(ch, step):
        for way in range(2):
            src, there = arrival(way, step)

            slot = gath[ch].at[src * 2 + core]
            on = there & has_next[way]

            def hop(step, way=way, slot=slot):
                return copy(slot, slot, ag_s.at[ch, way, step], ag_r.at[ch, way, step], next_id[way])

            def over(way=way, slot=slot):
                return copy(slot, slot, fw_s.at[ch, way, step], fw_r.at[ch, way, step], sib_id)

            pl.when(there)(lambda hop=hop: hop(step).wait_recv())
            if step + 1 < n_z - 1:
                send_when(on, functools.partial(hop, step + 1))
            send_when(there, over)

    def gathered(ch):
        for step in range(n_z - 1):
            for way in range(2):
                src, there = arrival(way, step)

                def come(way=way, step=step, src=src):
                    slot = gath[ch].at[src * 2 + 1 - core]
                    copy(slot, slot, fw_s.at[ch, way, step], fw_r.at[ch, way, step], sib_id).wait_recv()

                pl.when(there)(come)

    def contribute(ch):
        gathered(ch)
        if cap == group:
            rhs = jnp.concatenate([gath[ch][pos_ref[0, 0, k] // tbc] for k in range(cap)], axis=0)
            cbuf[ch] = jnp.dot(lhs[...], rhs, preferred_element_type=F32).astype(BF).reshape(n_row, rows, fc)
        else:
            acc_ref = lhs
            acc_ref[...] = jnp.zeros_like(acc_ref)

            def turn(t, carry):
                for i in range(group):
                    k = t * group + i
                    p = pos_ref[0, 0, k]
                    rhs = gath[ch][p // tbc]
                    prod = dot0(blk_v[k], rhs)
                    alive = k < live_ref[0, 0]
                    for j in range(tbc):
                        acc_ref[j * blk:(j + 1) * blk] += jnp.where(alive & (p % tbc == j), prod, 0.0)
                return carry

            lax.fori_loop(0, cap // group, turn, 0)
            cbuf[ch] = acc_ref[...].astype(BF).reshape(n_row, rows, fc)
        return [send(cbuf.at[ch, (me_r + d) % n_row], rbuf.at[ch, d - 1], c_s.at[ch, d - 1], c_r.at[ch, d - 1], row_id(d))
                for d in range(1, n_row)]

    total = None

    def project(ch, cps):
        for c in cps:
            c.wait_recv()
        s = cbuf[ch, me_r].astype(F32)
        for d in range(1, n_row):
            s += rbuf[ch, d - 1].astype(F32)
        return lax.dot_general(s.astype(BF), w_v[:, ch * fc:(ch + 1) * fc], (((1,), (1,)), ((), ())),
                               preferred_element_type=F32)

    base = core * half
    at_row = pl.ds(pl.multiple_of(base + me_r * piece, piece), piece)
    at_me = pl.ds(pl.multiple_of(base + me_r * piece + (z * part if scatter else 0), part), part)

    relay(0, 0)
    for ch in range(1, nch):
        depart(ch)

    loads[3].wait()
    if cap == group:
        for k in range(cap):
            at = pos_ref[0, 0, k] % tbc
            alive = k < live_ref[0, 0]
            turned = blk_v[k].T
            for j in range(tbc):
                lhs[j * blk:(j + 1) * blk, k * blk:(k + 1) * blk] = jnp.where(
                    alive & (at == j), turned, jnp.zeros((blk, blk), BF))

    for step in range(1, n_z - 2):
        relay(0, step)
    for c in g_cp:
        c.wait_recv()
    acc = gpart[me_r].astype(F32)
    for d in range(1, n_row):
        acc += grecv[d - 1].astype(F32)
    zsend[...] = acc.astype(BF).reshape(zsend.shape)
    zpick = [zsend.at[(z + d) % n_z if scatter else 0] for d in range(n_z)]
    zz_cp = [send(zpick[d], zrecv.at[d - 1], z_s.at[d - 1], z_r.at[d - 1], z_id(d)) for d in range(1, n_z)]

    def z_sum():
        for c in zz_cp:
            c.wait_recv()
        acc = zpick[0][...].astype(F32)
        for d in range(1, n_z):
            acc += zrecv[d - 1].astype(F32)
        gw[at_me] = acc.astype(BF)
        if not scatter:
            return []
        return [send(gw.at[at_me], gw.at[at_me], wz_s.at[d - 1], wz_r.at[d - 1], z_id(d)) for d in range(1, n_z)]

    lanes = 128
    if n_z > 2:
        relay(0, n_z - 2)
    for ch in range(1, nch):
        relay(ch, 0)
    c_cp = [contribute(0)]
    wz_cp = z_sum()
    for step in range(1, n_z - 1):
        for ch in range(1, nch):
            relay(ch, step)
    for c in wz_cp:
        c.wait_recv()
    wr_cp = [send(gw.at[at_row], gw.at[at_row], wr_s.at[d - 1], wr_r.at[d - 1], row_id(d)) for d in range(1, n_row)]
    wf_cp = [send(gw.at[at_row], gw.at[at_row], wf_s.at[0], wf_r.at[0], sib_id)]
    for ch in range(1, nch):
        c_cp.append(contribute(ch))

    bsend[...] = jnp.zeros_like(bsend)
    ones = jnp.ones((TILE, n_col * rows), BF)
    for ch in range(nch):
        sums = lax.dot_general(ones, gath[ch][...].reshape(n_col * rows, fc), (((1,), (0,)), ((), ())),
                               preferred_element_type=F32)
        for i in range(fc // lanes):
            at = ch * (fc // lanes) + i
            bsend[at:at + 1, :] = sums[0:1, i * lanes:(i + 1) * lanes]
    b_cp = [send(bsend, brecv.at[d - 1], b_s.at[d - 1], b_r.at[d - 1], row_id(d)) for d in range(1, n_row)]

    loads[4].wait()
    for ch in range(nch - 1):
        more = project(ch, c_cp[ch])
        total = more if total is None else total + more
    for d in range(1, n_row):
        wr_cp[d - 1].wait_recv()
        src = pl.ds(pl.multiple_of(base + ((me_r + n_row - d) % n_row) * piece, piece), piece)
        wf_cp.append(send(gw.at[src], gw.at[src], wf_s.at[d], wf_r.at[d], sib_id))
    gw_ref[mine] = gw[mine]
    more = project(nch - 1, c_cp[nch - 1])
    total = more if total is None else total + more
    gi_ref[...] = total.astype(BF)
    bias = bsend[...]
    for d in range(1, n_row):
        b_cp[d - 1].wait_recv()
        bias += brecv[d - 1]
    gb_ref[...] = bias
    for c in wf_cp:
        c.wait_recv()
    gw_ref[other] = gw[other]
    for now, make in sent:
        if now is None:
            make().wait_send()
        else:
            pl.when(now)(lambda make=make: make().wait_send())


def body(n_row, n_col, grad_out, relu_mask, aggregated, weight, adj_blocks, block_pos, block_live):
    rows, feat = grad_out.shape
    cap, blk = adj_blocks.shape[2], adj_blocks.shape[-1]
    group = max(d for d in range(1, 17) if cap % d == 0)
    nch = 2
    fc = feat // nch
    n_z = n_col // 2
    piece = feat // 2 // n_row
    scatter = piece % (n_z * TILE) == 0
    part = piece // n_z if scatter else piece
    tbc = n_row * rows // blk
    brows = -(-feat // 1024) * 8
    if cap == group:
        lhs = pltpu.VMEM((tbc * blk, cap * blk), BF)
    else:
        lhs = pltpu.VMEM((tbc * blk, fc), F32)
    dma = pltpu.SemaphoreType.DMA
    scratch = [pltpu.VMEM((n_col, rows, fc), BF) for _ in range(nch)] + [
        lhs,
        pltpu.VMEM((nch, n_row, rows, fc), BF),
        pltpu.VMEM((nch, n_row - 1, rows, fc), BF),
        pltpu.VMEM((rows, feat // 2), BF),
        pltpu.VMEM((n_row, piece, feat), BF),
        pltpu.VMEM((n_row - 1, piece, feat), BF),
        pltpu.VMEM((n_z if scatter else 1, part, feat), BF),
        pltpu.VMEM((n_z - 1, part, feat), BF),
        pltpu.VMEM((feat, feat), BF),
        pltpu.VMEM((rows, feat), BF),
        pltpu.VMEM((rows, feat), jnp.int32),
        pltpu.VMEM((rows, feat // 2), BF),
        pltpu.VMEM((feat, feat), BF),
        pltpu.VMEM((cap, blk, blk), BF),
        pltpu.VMEM((brows, 128), F32),
        pltpu.VMEM((n_row - 1, brows, 128), F32),
    ]
    sems = [dma((nch, 2, n_z - 1)), dma((nch, 2, n_z - 1)), dma((nch, 2, n_z - 1)), dma((nch, 2, n_z - 1)),
            dma((nch, n_row - 1)), dma((nch, n_row - 1)), dma(()), dma(()),
            dma((n_row - 1,)), dma((n_row - 1,)), dma((n_z - 1,)), dma((n_z - 1,)),
            dma((n_z - 1,)), dma((n_z - 1,)), dma((n_row - 1,)), dma((n_row - 1,)),
            dma((n_row,)), dma((n_row,)), dma((n_row - 1,)), dma((n_row - 1,)), dma((5,)),
            dma((nch,)), dma((nch,))]
    vm = pl.BlockSpec(memory_space=pltpu.VMEM)
    hbm = pl.BlockSpec(memory_space=pltpu.HBM)
    sm = pl.BlockSpec(memory_space=pltpu.SMEM)
    gi, gw, gb = pl.pallas_call(
        functools.partial(kernel, (n_row, n_col, nch, cap, group, scatter)),
        out_shape=(jax.ShapeDtypeStruct((rows, feat), BF),
                   jax.ShapeDtypeStruct((feat, feat), BF),
                   jax.ShapeDtypeStruct((brows, 128), F32)),
        in_specs=[hbm, hbm, hbm, hbm, hbm, sm, sm],
        out_specs=(vm, vm, vm),
        scratch_shapes=scratch + sems,
        compiler_params=pltpu.CompilerParams(collective_id=0, has_side_effects=True,
                                             vmem_limit_bytes=(8 if cap == group else 48) * 1024 * 1024),
    )(*(pltpu.with_memory_space_constraint(x, pltpu.HBM)
        for x in (grad_out, relu_mask, aggregated, weight, adj_blocks)), block_pos, block_live)
    factor = 1.0 / math.sqrt(rows * n_row * n_col)
    return gi.reshape(1, rows, feat), gw.astype(F32) * factor, gb.reshape(-1)[:feat] * factor


def solution(mesh):
    return jax.shard_map(
        functools.partial(body, mesh.shape["row"], mesh.shape["col"]),
        mesh=mesh,
        in_specs=(
            P(("row", "col"), None),
            P(("row", "col"), None),
            P(("row", "col"), None),
            P(),
            P("row", "col", None, None, None),
            P("row", "col", None),
            P("row", "col"),
        ),
        out_specs=(P("col", "row", None), P(), P()),
        check_vma=False,
    )
```

```python
import functools
import math

import jax
import jax.numpy as jnp
from jax import lax
from jax.experimental import pallas as pl
from jax.experimental.pallas import tpu as pltpu
from jax.sharding import PartitionSpec as P

MESH = pl.DeviceIdType.MESH
BF = jnp.bfloat16
F32 = jnp.float32
TILE = 16


def dot0(a, b):
    return lax.dot_general(a, b, (((0,), (0,)), ((), ())), preferred_element_type=F32)


def kernel(cfg, go_ref, mask_ref, agg_ref, w_ref, blk_ref, pos_ref, live_ref,
           gi_ref, gw_ref, gb_ref, *scr):
    n_row, n_col, nch, cap, group, scatter = cfg
    n_z = n_col // 2
    gath = scr[:nch]
    lhs, cbuf, rbuf, asib, gpart, grecv, zsend, zrecv, gw, go_v, mask_v, agg_v, w_v, blk_v, bsend, brecv = scr[nch:nch + 16]
    (ag_s, ag_r, fw_s, fw_r, c_s, c_r, as_s, as_r, g_s, g_r, z_s, z_r, wz_s, wz_r, wr_s, wr_r, wf_s, wf_r,
     b_s, b_r, in_s, sb_s, sb_r) = scr[nch + 16:]
    rows, feat = go_ref.shape
    fc = feat // nch
    blk = blk_ref.shape[-1]
    tbc = n_row * rows // blk
    half = feat // 2
    piece = half // n_row
    part = piece // n_z if scatter else piece
    me_r, me_c = lax.axis_index("row"), lax.axis_index("col")
    z, core = me_c // 2, me_c % 2
    sib = z * 2 + 1 - core
    sib_id = (me_r, sib)

    def row_id(d):
        return ((me_r + d) % n_row, me_c)

    def z_id(d):
        return (me_r, ((z + d) % n_z) * 2 + core)

    other = pl.ds(pl.multiple_of((1 - core) * half, half), half)
    mine = pl.ds(pl.multiple_of(core * half, half), half)
    loads = [pltpu.make_async_copy(src, dst, in_s.at[i]) for i, (src, dst) in enumerate((
        (go_ref, go_v), (mask_ref, mask_v), (agg_ref.at[:, mine], agg_v), (blk_ref.at[0, 0], blk_v), (w_ref, w_v)))]
    for c in loads:
        c.start()

    sent = []

    def copy(src, dst, s, r, dev):
        return pltpu.make_async_remote_copy(src_ref=src, dst_ref=dst, send_sem=s, recv_sem=r,
                                               device_id=dev, device_id_type=MESH)

    def send(*what):
        c = copy(*what)
        c.start()
        sent.append((None, lambda: copy(*what)))
        return c

    def send_when(now, make):
        pl.when(now)(lambda: make().start())
        sent.append((now, make))

    barrier = pltpu.get_barrier_semaphore()
    peers = [sib_id] + [z_id(d) for d in range(1, n_z)] + [row_id(d) for d in range(1, n_row)]
    for p in peers:
        pl.semaphore_signal(barrier, inc=1, device_id=p, device_id_type=MESH)

    loads[0].wait()
    loads[1].wait()
    for ch in range(nch):
        cols = slice(ch * fc, (ch + 1) * fc)
        gath[ch][me_c] = go_v[:, cols] * mask_v[:, cols].astype(F32).astype(BF)

    pl.semaphore_wait(barrier, len(peers))

    has_next = (z < n_z - 1, z > 0)
    next_id = ((me_r, me_c + 2), (me_r, me_c - 2))
    sib_cp = []
    agg_cp = send(agg_ref.at[:, other], asib, as_s, as_r, sib_id)
    for ch in range(nch):
        own = gath[ch].at[me_c]
        sib_cp.append(send(own, own, sb_s.at[ch], sb_r.at[ch], sib_id))

    def depart(ch):
        own = gath[ch].at[me_c]
        for way in range(2):
            send_when(has_next[way], lambda way=way: copy(
                own, own, ag_s.at[ch, way, 0], ag_r.at[ch, way, 0], next_id[way]))

    for ch in range(2):
        depart(ch)

    loads[2].wait()
    agg_cp.wait_recv()
    for ch in range(nch):
        cols = slice(ch * fc, (ch + 1) * fc)
        sib_cp[ch].wait_recv()
        g = dot0(agg_v[...], gath[ch][me_c]) + dot0(asib[...], gath[ch][sib])
        gpart[:, :, cols] = g.astype(BF).reshape(n_row, piece, fc)
    g_cp = [send(gpart.at[(me_r + d) % n_row], grecv.at[d - 1], g_s.at[d - 1], g_r.at[d - 1], row_id(d))
            for d in range(1, n_row)]

    def arrival(way, step):
        src = z - 1 - step if way == 0 else z + 1 + step
        return src, (src >= 0 if way == 0 else src <= n_z - 1)

    def relay(ch, step):
        for way in range(2):
            src, there = arrival(way, step)

            slot = gath[ch].at[src * 2 + core]
            on = there & has_next[way]

            def hop(step, way=way, slot=slot):
                return copy(slot, slot, ag_s.at[ch, way, step], ag_r.at[ch, way, step], next_id[way])

            def over(way=way, slot=slot):
                return copy(slot, slot, fw_s.at[ch, way, step], fw_r.at[ch, way, step], sib_id)

            pl.when(there)(lambda hop=hop: hop(step).wait_recv())
            if step + 1 < n_z - 1:
                send_when(on, functools.partial(hop, step + 1))
            send_when(there, over)

    def gathered(ch):
        for step in range(n_z - 1):
            for way in range(2):
                src, there = arrival(way, step)

                def come(way=way, step=step, src=src):
                    slot = gath[ch].at[src * 2 + 1 - core]
                    copy(slot, slot, fw_s.at[ch, way, step], fw_r.at[ch, way, step], sib_id).wait_recv()

                pl.when(there)(come)

    lanes = 128
    ones = jnp.ones((TILE, n_col * rows), BF)
    bsend[...] = jnp.zeros_like(bsend)

    def contribute(ch):
        gathered(ch)
        if cap == group:
            rhs = jnp.concatenate([gath[ch][pos_ref[0, 0, k] // tbc] for k in range(cap)], axis=0)
            cbuf[ch] = jnp.dot(lhs[...], rhs, preferred_element_type=F32).astype(BF).reshape(n_row, rows, fc)
        else:
            acc_ref = lhs
            acc_ref[...] = jnp.zeros_like(acc_ref)

            def turn(t, carry):
                for i in range(group):
                    k = t * group + i
                    p = pos_ref[0, 0, k]
                    rhs = gath[ch][p // tbc]
                    prod = dot0(blk_v[k], rhs)
                    alive = k < live_ref[0, 0]
                    for j in range(tbc):
                        acc_ref[j * blk:(j + 1) * blk] += jnp.where(alive & (p % tbc == j), prod, 0.0)
                return carry

            lax.fori_loop(0, cap // group, turn, 0)
            cbuf[ch] = acc_ref[...].astype(BF).reshape(n_row, rows, fc)
        cps = [send(cbuf.at[ch, (me_r + d) % n_row], rbuf.at[ch, d - 1], c_s.at[ch, d - 1], c_r.at[ch, d - 1], row_id(d))
               for d in range(1, n_row)]
        sums = lax.dot_general(ones, gath[ch][...].reshape(n_col * rows, fc), (((1,), (0,)), ((), ())),
                               preferred_element_type=F32)
        for i in range(fc // lanes):
            at = ch * (fc // lanes) + i
            bsend[at:at + 1, :] = sums[0:1, i * lanes:(i + 1) * lanes]
        return cps

    total = None

    def project(ch, cps):
        for c in cps:
            c.wait_recv()
        s = cbuf[ch, me_r].astype(F32)
        for d in range(1, n_row):
            s += rbuf[ch, d - 1].astype(F32)
        return lax.dot_general(s.astype(BF), w_v[:, ch * fc:(ch + 1) * fc], (((1,), (1,)), ((), ())),
                               preferred_element_type=F32)

    base = core * half
    at_row = pl.ds(pl.multiple_of(base + me_r * piece, piece), piece)
    at_me = pl.ds(pl.multiple_of(base + me_r * piece + (z * part if scatter else 0), part), part)

    def spread():
        loads[3].wait()
        if cap == group:
            for k in range(cap):
                at = pos_ref[0, 0, k] % tbc
                alive = k < live_ref[0, 0]
                turned = blk_v[k].T
                for j in range(tbc):
                    lhs[j * blk:(j + 1) * blk, k * blk:(k + 1) * blk] = jnp.where(
                        alive & (at == j), turned, jnp.zeros((blk, blk), BF))

    zpick = [zsend.at[(z + d) % n_z if scatter else 0] for d in range(n_z)]
    zz_cp, wz_cp, wr_cp, wf_cp = [], [], [], []

    def row_sum():
        for c in g_cp:
            c.wait_recv()
        acc = gpart[me_r].astype(F32)
        for d in range(1, n_row):
            acc += grecv[d - 1].astype(F32)
        zsend[...] = acc.astype(BF).reshape(zsend.shape)
        for d in range(1, n_z):
            zz_cp.append(send(zpick[d], zrecv.at[d - 1], z_s.at[d - 1], z_r.at[d - 1], z_id(d)))

    def z_sum():
        for c in zz_cp:
            c.wait_recv()
        acc = zpick[0][...].astype(F32)
        for d in range(1, n_z):
            acc += zrecv[d - 1].astype(F32)
        gw[at_me] = acc.astype(BF)
        if scatter:
            for d in range(1, n_z):
                wz_cp.append(send(gw.at[at_me], gw.at[at_me], wz_s.at[d - 1], wz_r.at[d - 1], z_id(d)))

    def row_gather():
        for c in wz_cp:
            c.wait_recv()
        for d in range(1, n_row):
            wr_cp.append(send(gw.at[at_row], gw.at[at_row], wr_s.at[d - 1], wr_r.at[d - 1], row_id(d)))
        wf_cp.append(send(gw.at[at_row], gw.at[at_row], wf_s.at[0], wf_r.at[0], sib_id))

    c_cp = []
    todo = []
    for ch in range(nch):
        at = 1.9 * (ch // 2) + 0.1 * ch
        if ch >= 2:
            todo.append((at - 1.6 + 0.8 * (ch % 2), functools.partial(depart, ch)))
        for step in range(n_z - 1):
            todo.append((at + step, functools.partial(relay, ch, step)))
        todo.append((at + n_z - 2 + 0.85, lambda ch=ch: c_cp.append(contribute(ch))))
    todo += [(0.7, spread), (1.6, row_sum), (n_z - 0.91, z_sum), (n_z + 0.6, row_gather)]
    for _, act in sorted(todo, key=lambda item: item[0]):
        act()

    b_cp = [send(bsend, brecv.at[d - 1], b_s.at[d - 1], b_r.at[d - 1], row_id(d)) for d in range(1, n_row)]

    loads[4].wait()
    for ch in range(nch - 2):
        more = project(ch, c_cp[ch])
        total = more if total is None else total + more
    for d in range(1, n_row):
        wr_cp[d - 1].wait_recv()
        src = pl.ds(pl.multiple_of(base + ((me_r + n_row - d) % n_row) * piece, piece), piece)
        wf_cp.append(send(gw.at[src], gw.at[src], wf_s.at[d], wf_r.at[d], sib_id))
    gw_ref[mine] = gw[mine]
    for ch in range(nch - 2, nch):
        more = project(ch, c_cp[ch])
        total = more if total is None else total + more
    gi_ref[...] = total.astype(BF)
    bias = bsend[...]
    for d in range(1, n_row):
        b_cp[d - 1].wait_recv()
        bias += brecv[d - 1]
    gb_ref[...] = bias
    for c in wf_cp:
        c.wait_recv()
    gw_ref[other] = gw[other]
    for now, make in sent:
        if now is None:
            make().wait_send()
        else:
            pl.when(now)(lambda make=make: make().wait_send())


def body(n_row, n_col, grad_out, relu_mask, aggregated, weight, adj_blocks, block_pos, block_live):
    rows, feat = grad_out.shape
    cap, blk = adj_blocks.shape[2], adj_blocks.shape[-1]
    group = max(d for d in range(1, 17) if cap % d == 0)
    nch = 4
    fc = feat // nch
    n_z = n_col // 2
    piece = feat // 2 // n_row
    scatter = piece % (n_z * TILE) == 0
    part = piece // n_z if scatter else piece
    tbc = n_row * rows // blk
    brows = -(-feat // 1024) * 8
    if cap == group:
        lhs = pltpu.VMEM((tbc * blk, cap * blk), BF)
    else:
        lhs = pltpu.VMEM((tbc * blk, fc), F32)
    dma = pltpu.SemaphoreType.DMA
    scratch = [pltpu.VMEM((n_col, rows, fc), BF) for _ in range(nch)] + [
        lhs,
        pltpu.VMEM((nch, n_row, rows, fc), BF),
        pltpu.VMEM((nch, n_row - 1, rows, fc), BF),
        pltpu.VMEM((rows, feat // 2), BF),
        pltpu.VMEM((n_row, piece, feat), BF),
        pltpu.VMEM((n_row - 1, piece, feat), BF),
        pltpu.VMEM((n_z if scatter else 1, part, feat), BF),
        pltpu.VMEM((n_z - 1, part, feat), BF),
        pltpu.VMEM((feat, feat), BF),
        pltpu.VMEM((rows, feat), BF),
        pltpu.VMEM((rows, feat), jnp.int32),
        pltpu.VMEM((rows, feat // 2), BF),
        pltpu.VMEM((feat, feat), BF),
        pltpu.VMEM((cap, blk, blk), BF),
        pltpu.VMEM((brows, 128), F32),
        pltpu.VMEM((n_row - 1, brows, 128), F32),
    ]
    sems = [dma((nch, 2, n_z - 1)), dma((nch, 2, n_z - 1)), dma((nch, 2, n_z - 1)), dma((nch, 2, n_z - 1)),
            dma((nch, n_row - 1)), dma((nch, n_row - 1)), dma(()), dma(()),
            dma((n_row - 1,)), dma((n_row - 1,)), dma((n_z - 1,)), dma((n_z - 1,)),
            dma((n_z - 1,)), dma((n_z - 1,)), dma((n_row - 1,)), dma((n_row - 1,)),
            dma((n_row,)), dma((n_row,)), dma((n_row - 1,)), dma((n_row - 1,)), dma((5,)),
            dma((nch,)), dma((nch,))]
    vm = pl.BlockSpec(memory_space=pltpu.VMEM)
    hbm = pl.BlockSpec(memory_space=pltpu.HBM)
    sm = pl.BlockSpec(memory_space=pltpu.SMEM)
    gi, gw, gb = pl.pallas_call(
        functools.partial(kernel, (n_row, n_col, nch, cap, group, scatter)),
        out_shape=(jax.ShapeDtypeStruct((rows, feat), BF),
                   jax.ShapeDtypeStruct((feat, feat), BF),
                   jax.ShapeDtypeStruct((brows, 128), F32)),
        in_specs=[hbm, hbm, hbm, hbm, hbm, sm, sm],
        out_specs=(vm, vm, vm),
        scratch_shapes=scratch + sems,
        compiler_params=pltpu.CompilerParams(collective_id=0, has_side_effects=True,
                                             vmem_limit_bytes=(8 if cap == group else 48) * 1024 * 1024),
    )(*(pltpu.with_memory_space_constraint(x, pltpu.HBM)
        for x in (grad_out, relu_mask, aggregated, weight, adj_blocks)), block_pos, block_live)
    factor = 1.0 / math.sqrt(rows * n_row * n_col)
    return gi.reshape(1, rows, feat), gw.astype(F32) * factor, gb.reshape(-1)[:feat] * factor


def solution(mesh):
    return jax.shard_map(
        functools.partial(body, mesh.shape["row"], mesh.shape["col"]),
        mesh=mesh,
        in_specs=(
            P(("row", "col"), None),
            P(("row", "col"), None),
            P(("row", "col"), None),
            P(),
            P("row", "col", None, None, None),
            P("row", "col", None),
            P("row", "col"),
        ),
        out_specs=(P("col", "row", None), P(), P()),
        check_vma=False,
    )
```

```python
import functools
import math

import jax
import jax.numpy as jnp
from jax import lax
from jax.experimental import pallas as pl
from jax.experimental.pallas import tpu as pltpu
from jax.sharding import PartitionSpec as P

MESH = pl.DeviceIdType.MESH
BF = jnp.bfloat16
F32 = jnp.float32
TILE = 16


def dot0(a, b):
    return lax.dot_general(a, b, (((0,), (0,)), ((), ())), preferred_element_type=F32)


def kernel(cfg, go_ref, mask_ref, agg_ref, w_ref, blk_ref, pos_ref, live_ref,
           gi_ref, gw_ref, gb_ref, *scr):
    n_row, n_col, nch, cap, group, scatter = cfg
    n_z = n_col // 2
    gath = scr[:nch]
    lhs, cbuf, rbuf, asib, gpart, grecv, zsend, zrecv, gw, go_v, mask_v, agg_v, w_v, blk_v, bsend, brecv, w_t = scr[nch:nch + 17]
    (ag_s, ag_r, fw_s, fw_r, c_s, c_r, as_s, as_r, g_s, g_r, z_s, z_r, wz_s, wz_r, wr_s, wr_r, wf_s, wf_r,
     b_s, b_r, in_s, sb_s, sb_r) = scr[nch + 17:]
    rows, feat = go_ref.shape
    fc = feat // nch
    blk = blk_ref.shape[-1]
    tbc = n_row * rows // blk
    half = feat // 2
    piece = half // n_row
    part = piece // n_z if scatter else piece
    me_r, me_c = lax.axis_index("row"), lax.axis_index("col")
    z, core = me_c // 2, me_c % 2
    sib = z * 2 + 1 - core
    sib_id = (me_r, sib)

    def row_id(d):
        return ((me_r + d) % n_row, me_c)

    def z_id(d):
        return (me_r, ((z + d) % n_z) * 2 + core)

    other = pl.ds(pl.multiple_of((1 - core) * half, half), half)
    mine = pl.ds(pl.multiple_of(core * half, half), half)
    loads = [pltpu.make_async_copy(src, dst, in_s.at[i]) for i, (src, dst) in enumerate((
        (go_ref, go_v), (mask_ref, mask_v), (agg_ref.at[:, mine], agg_v), (blk_ref.at[0, 0], blk_v), (w_ref, w_v)))]
    for c in loads:
        c.start()

    sent = []

    def copy(src, dst, s, r, dev):
        return pltpu.make_async_remote_copy(src_ref=src, dst_ref=dst, send_sem=s, recv_sem=r,
                                               device_id=dev, device_id_type=MESH)

    def send(*what):
        c = copy(*what)
        c.start()
        sent.append((None, lambda: copy(*what)))
        return c

    def send_when(now, make):
        pl.when(now)(lambda: make().start())
        sent.append((now, make))

    barrier = pltpu.get_barrier_semaphore()
    peers = [sib_id] + [z_id(d) for d in range(1, n_z)] + [row_id(d) for d in range(1, n_row)]
    for p in peers:
        pl.semaphore_signal(barrier, inc=1, device_id=p, device_id_type=MESH)

    loads[0].wait()
    loads[1].wait()
    for ch in range(nch):
        cols = slice(ch * fc, (ch + 1) * fc)
        gath[ch][me_c] = go_v[:, cols] * mask_v[:, cols].astype(F32).astype(BF)

    pl.semaphore_wait(barrier, len(peers))

    has_next = (z < n_z - 1, z > 0)
    next_id = ((me_r, me_c + 2), (me_r, me_c - 2))
    sib_cp = []
    agg_cp = send(agg_ref.at[:, other], asib, as_s, as_r, sib_id)
    for ch in range(nch):
        own = gath[ch].at[me_c]
        sib_cp.append(send(own, own, sb_s.at[ch], sb_r.at[ch], sib_id))

    def depart(ch):
        own = gath[ch].at[me_c]
        for way in range(2):
            send_when(has_next[way], lambda way=way: copy(
                own, own, ag_s.at[ch, way, 0], ag_r.at[ch, way, 0], next_id[way]))

    depart(0)

    loads[2].wait()
    agg_cp.wait_recv()
    for ch in range(nch):
        cols = slice(ch * fc, (ch + 1) * fc)
        sib_cp[ch].wait_recv()
        g = dot0(agg_v[...], gath[ch][me_c]) + dot0(asib[...], gath[ch][sib])
        gpart[:, :, cols] = g.astype(BF).reshape(n_row, piece, fc)
    g_cp = [send(gpart.at[(me_r + d) % n_row], grecv.at[d - 1], g_s.at[d - 1], g_r.at[d - 1], row_id(d))
            for d in range(1, n_row)]

    def arrival(way, step):
        src = z - 1 - step if way == 0 else z + 1 + step
        return src, (src >= 0 if way == 0 else src <= n_z - 1)

    def relay(ch, step):
        for way in range(2):
            src, there = arrival(way, step)

            slot = gath[ch].at[src * 2 + core]
            on = there & has_next[way]

            def hop(step, way=way, slot=slot):
                return copy(slot, slot, ag_s.at[ch, way, step], ag_r.at[ch, way, step], next_id[way])

            def over(way=way, slot=slot):
                return copy(slot, slot, fw_s.at[ch, way, step], fw_r.at[ch, way, step], sib_id)

            pl.when(there)(lambda hop=hop: hop(step).wait_recv())
            if step + 1 < n_z - 1:
                send_when(on, functools.partial(hop, step + 1))
            send_when(there, over)

    def gathered(ch):
        for step in range(n_z - 1):
            for way in range(2):
                src, there = arrival(way, step)

                def come(way=way, step=step, src=src):
                    slot = gath[ch].at[src * 2 + 1 - core]
                    copy(slot, slot, fw_s.at[ch, way, step], fw_r.at[ch, way, step], sib_id).wait_recv()

                pl.when(there)(come)

    lanes = 128
    ones = jnp.ones((TILE, n_col * rows), BF)
    bsend[...] = jnp.zeros_like(bsend)

    def contribute(ch):
        gathered(ch)
        if cap == group:
            rhs = jnp.concatenate([gath[ch][pos_ref[0, 0, k] // tbc] for k in range(cap)], axis=0)
            cbuf[ch] = jnp.dot(lhs[...], rhs, preferred_element_type=F32).astype(BF).reshape(n_row, rows, fc)
        else:
            acc_ref = lhs
            acc_ref[...] = jnp.zeros_like(acc_ref)

            def turn(t, carry):
                for i in range(group):
                    k = t * group + i
                    p = pos_ref[0, 0, k]
                    rhs = gath[ch][p // tbc]
                    prod = dot0(blk_v[k], rhs)
                    alive = k < live_ref[0, 0]
                    for j in range(tbc):
                        acc_ref[j * blk:(j + 1) * blk] += jnp.where(alive & (p % tbc == j), prod, 0.0)
                return carry

            lax.fori_loop(0, cap // group, turn, 0)
            cbuf[ch] = acc_ref[...].astype(BF).reshape(n_row, rows, fc)
        cps = [send(cbuf.at[ch, (me_r + d) % n_row], rbuf.at[ch, d - 1], c_s.at[ch, d - 1], c_r.at[ch, d - 1], row_id(d))
               for d in range(1, n_row)]
        return cps

    total = None

    def project(ch, cps):
        for c in cps:
            c.wait_recv()
        s = cbuf[ch, me_r].astype(F32)
        for d in range(1, n_row):
            s += rbuf[ch, d - 1].astype(F32)
        return jnp.dot(s.astype(BF), w_t[ch * fc:(ch + 1) * fc], preferred_element_type=F32)

    def turn_weight():
        loads[4].wait()
        w_t[...] = w_v[...].T

    base = core * half
    at_row = pl.ds(pl.multiple_of(base + me_r * piece, piece), piece)
    at_me = pl.ds(pl.multiple_of(base + me_r * piece + (z * part if scatter else 0), part), part)

    def spread():
        loads[3].wait()
        if cap == group:
            for k in range(cap):
                at = pos_ref[0, 0, k] % tbc
                alive = k < live_ref[0, 0]
                turned = blk_v[k].T
                for j in range(tbc):
                    lhs[j * blk:(j + 1) * blk, k * blk:(k + 1) * blk] = jnp.where(
                        alive & (at == j), turned, jnp.zeros((blk, blk), BF))

    zpick = [zsend.at[(z + d) % n_z if scatter else 0] for d in range(n_z)]
    zz_cp, wz_cp, wr_cp, wf_cp = [], [], [], []

    def row_sum():
        for c in g_cp:
            c.wait_recv()
        acc = gpart[me_r].astype(F32)
        for d in range(1, n_row):
            acc += grecv[d - 1].astype(F32)
        zsend[...] = acc.astype(BF).reshape(zsend.shape)
        for d in range(1, n_z):
            zz_cp.append(send(zpick[d], zrecv.at[d - 1], z_s.at[d - 1], z_r.at[d - 1], z_id(d)))

    def z_sum():
        for c in zz_cp:
            c.wait_recv()
        acc = zpick[0][...].astype(F32)
        for d in range(1, n_z):
            acc += zrecv[d - 1].astype(F32)
        gw[at_me] = acc.astype(BF)
        if scatter:
            for d in range(1, n_z):
                wz_cp.append(send(gw.at[at_me], gw.at[at_me], wz_s.at[d - 1], wz_r.at[d - 1], z_id(d)))

    def row_gather():
        for c in wz_cp:
            c.wait_recv()
        for d in range(1, n_row):
            wr_cp.append(send(gw.at[at_row], gw.at[at_row], wr_s.at[d - 1], wr_r.at[d - 1], row_id(d)))
        wf_cp.append(send(gw.at[at_row], gw.at[at_row], wf_s.at[0], wf_r.at[0], sib_id))

    c_cp = []
    todo = []
    for ch in range(nch):
        at = 1.9 * ch
        if ch >= 1:
            todo.append((at - 1.4, functools.partial(depart, ch)))
        for step in range(n_z - 1):
            todo.append((at + step, functools.partial(relay, ch, step)))
        todo.append((at + n_z - 2 + 0.85, lambda ch=ch: c_cp.append(contribute(ch))))
    todo += [(0.7, spread), (1.6, row_sum), (n_z - 1.5, z_sum), (n_z - 1.05, turn_weight), (n_z - 0.5, row_gather)]
    for _, act in sorted(todo, key=lambda item: item[0]):
        act()

    for ch in range(nch):
        sums = lax.dot_general(ones, gath[ch][...].reshape(n_col * rows, fc), (((1,), (0,)), ((), ())),
                               preferred_element_type=F32)
        for i in range(fc // lanes):
            at = ch * (fc // lanes) + i
            bsend[at:at + 1, :] = sums[0:1, i * lanes:(i + 1) * lanes]
    b_cp = [send(bsend, brecv.at[d - 1], b_s.at[d - 1], b_r.at[d - 1], row_id(d)) for d in range(1, n_row)]

    for ch in range(nch - 1):
        more = project(ch, c_cp[ch])
        total = more if total is None else total + more
    for d in range(1, n_row):
        wr_cp[d - 1].wait_recv()
        src = pl.ds(pl.multiple_of(base + ((me_r + n_row - d) % n_row) * piece, piece), piece)
        wf_cp.append(send(gw.at[src], gw.at[src], wf_s.at[d], wf_r.at[d], sib_id))
    gw_ref[mine] = gw[mine]
    for ch in range(nch - 1, nch):
        more = project(ch, c_cp[ch])
        total = more if total is None else total + more
    gi_ref[...] = total.astype(BF)
    bias = bsend[...]
    for d in range(1, n_row):
        b_cp[d - 1].wait_recv()
        bias += brecv[d - 1]
    gb_ref[...] = bias
    for c in wf_cp:
        c.wait_recv()
    gw_ref[other] = gw[other]
    for now, make in sent:
        if now is None:
            make().wait_send()
        else:
            pl.when(now)(lambda make=make: make().wait_send())


def body(n_row, n_col, grad_out, relu_mask, aggregated, weight, adj_blocks, block_pos, block_live):
    rows, feat = grad_out.shape
    cap, blk = adj_blocks.shape[2], adj_blocks.shape[-1]
    group = max(d for d in range(1, 17) if cap % d == 0)
    nch = 2
    fc = feat // nch
    n_z = n_col // 2
    piece = feat // 2 // n_row
    scatter = piece % (n_z * TILE) == 0
    part = piece // n_z if scatter else piece
    tbc = n_row * rows // blk
    brows = -(-feat // 1024) * 8
    if cap == group:
        lhs = pltpu.VMEM((tbc * blk, cap * blk), BF)
    else:
        lhs = pltpu.VMEM((tbc * blk, fc), F32)
    dma = pltpu.SemaphoreType.DMA
    scratch = [pltpu.VMEM((n_col, rows, fc), BF) for _ in range(nch)] + [
        lhs,
        pltpu.VMEM((nch, n_row, rows, fc), BF),
        pltpu.VMEM((nch, n_row - 1, rows, fc), BF),
        pltpu.VMEM((rows, feat // 2), BF),
        pltpu.VMEM((n_row, piece, feat), BF),
        pltpu.VMEM((n_row - 1, piece, feat), BF),
        pltpu.VMEM((n_z if scatter else 1, part, feat), BF),
        pltpu.VMEM((n_z - 1, part, feat), BF),
        pltpu.VMEM((feat, feat), BF),
        pltpu.VMEM((rows, feat), BF),
        pltpu.VMEM((rows, feat), jnp.int32),
        pltpu.VMEM((rows, feat // 2), BF),
        pltpu.VMEM((feat, feat), BF),
        pltpu.VMEM((cap, blk, blk), BF),
        pltpu.VMEM((brows, 128), F32),
        pltpu.VMEM((n_row - 1, brows, 128), F32),
        pltpu.VMEM((feat, feat), BF),
    ]
    sems = [dma((nch, 2, n_z - 1)), dma((nch, 2, n_z - 1)), dma((nch, 2, n_z - 1)), dma((nch, 2, n_z - 1)),
            dma((nch, n_row - 1)), dma((nch, n_row - 1)), dma(()), dma(()),
            dma((n_row - 1,)), dma((n_row - 1,)), dma((n_z - 1,)), dma((n_z - 1,)),
            dma((n_z - 1,)), dma((n_z - 1,)), dma((n_row - 1,)), dma((n_row - 1,)),
            dma((n_row,)), dma((n_row,)), dma((n_row - 1,)), dma((n_row - 1,)), dma((5,)),
            dma((nch,)), dma((nch,))]
    vm = pl.BlockSpec(memory_space=pltpu.VMEM)
    hbm = pl.BlockSpec(memory_space=pltpu.HBM)
    sm = pl.BlockSpec(memory_space=pltpu.SMEM)
    gi, gw, gb = pl.pallas_call(
        functools.partial(kernel, (n_row, n_col, nch, cap, group, scatter)),
        out_shape=(jax.ShapeDtypeStruct((rows, feat), BF),
                   jax.ShapeDtypeStruct((feat, feat), BF),
                   jax.ShapeDtypeStruct((brows, 128), F32)),
        in_specs=[hbm, hbm, hbm, hbm, hbm, sm, sm],
        out_specs=(vm, vm, vm),
        scratch_shapes=scratch + sems,
        compiler_params=pltpu.CompilerParams(collective_id=0, has_side_effects=True,
                                             vmem_limit_bytes=(8 if cap == group else 48) * 1024 * 1024),
    )(*(pltpu.with_memory_space_constraint(x, pltpu.HBM)
        for x in (grad_out, relu_mask, aggregated, weight, adj_blocks)), block_pos, block_live)
    factor = 1.0 / math.sqrt(rows * n_row * n_col)
    return gi.reshape(1, rows, feat), gw.astype(F32) * factor, gb.reshape(-1)[:feat] * factor


def solution(mesh):
    return jax.shard_map(
        functools.partial(body, mesh.shape["row"], mesh.shape["col"]),
        mesh=mesh,
        in_specs=(
            P(("row", "col"), None),
            P(("row", "col"), None),
            P(("row", "col"), None),
            P(),
            P("row", "col", None, None, None),
            P("row", "col", None),
            P("row", "col"),
        ),
        out_specs=(P("col", "row", None), P(), P()),
        check_vma=False,
    )
```

```python
import functools
import math

import jax
import jax.numpy as jnp
from jax import lax
from jax.experimental import pallas as pl
from jax.experimental.pallas import tpu as pltpu
from jax.sharding import PartitionSpec as P

MESH = pl.DeviceIdType.MESH
BF = jnp.bfloat16
F32 = jnp.float32
TILE = 16


def dot0(a, b):
    return lax.dot_general(a, b, (((0,), (0,)), ((), ())), preferred_element_type=F32)


def kernel(cfg, go_ref, mask_ref, agg_ref, w_ref, blk_ref, pos_ref, live_ref,
           gi_ref, gw_ref, gb_ref, *scr):
    n_row, n_col, nch, cap, group, scatter = cfg
    n_z = n_col // 2
    gath = scr[:nch]
    lhs, cbuf, rbuf, asib, gpart, grecv, zsend, zrecv, gw, go_v, mask_v, agg_v, w_v, blk_v, bsend, brecv, w_t = scr[nch:nch + 17]
    (ag_s, ag_r, fw_s, fw_r, c_s, c_r, as_s, as_r, g_s, g_r, z_s, z_r, wz_s, wz_r, wr_s, wr_r, wf_s, wf_r,
     b_s, b_r, in_s, sb_s, sb_r) = scr[nch + 17:]
    rows, feat = go_ref.shape
    fc = feat // nch
    blk = blk_ref.shape[-1]
    tbc = n_row * rows // blk
    half = feat // 2
    piece = half // n_row
    part = piece // n_z if scatter else piece
    me_r, me_c = lax.axis_index("row"), lax.axis_index("col")
    z, core = me_c // 2, me_c % 2
    sib = z * 2 + 1 - core
    sib_id = (me_r, sib)

    def row_id(d):
        return ((me_r + d) % n_row, me_c)

    def z_id(d):
        return (me_r, ((z + d) % n_z) * 2 + core)

    other = pl.ds(pl.multiple_of((1 - core) * half, half), half)
    mine = pl.ds(pl.multiple_of(core * half, half), half)
    loads = [pltpu.make_async_copy(src, dst, in_s.at[i]) for i, (src, dst) in enumerate((
        (go_ref, go_v), (mask_ref, mask_v), (agg_ref.at[:, mine], agg_v), (blk_ref.at[0, 0], blk_v), (w_ref, w_v)))]
    for c in loads:
        c.start()

    sent = []

    def copy(src, dst, s, r, dev):
        return pltpu.make_async_remote_copy(src_ref=src, dst_ref=dst, send_sem=s, recv_sem=r,
                                               device_id=dev, device_id_type=MESH)

    def send(*what):
        c = copy(*what)
        c.start()
        sent.append((None, lambda: copy(*what)))
        return c

    def send_when(now, make):
        pl.when(now)(lambda: make().start())
        sent.append((now, make))

    barrier = pltpu.get_barrier_semaphore()
    peers = [sib_id] + [z_id(d) for d in range(1, n_z)] + [row_id(d) for d in range(1, n_row)]
    for p in peers:
        pl.semaphore_signal(barrier, inc=1, device_id=p, device_id_type=MESH)

    loads[0].wait()
    loads[1].wait()
    for ch in range(nch):
        cols = slice(ch * fc, (ch + 1) * fc)
        gath[ch][me_c] = go_v[:, cols] * mask_v[:, cols].astype(F32).astype(BF)

    pl.semaphore_wait(barrier, len(peers))

    has_next = (z < n_z - 1, z > 0)
    next_id = ((me_r, me_c + 2), (me_r, me_c - 2))
    sib_cp = []
    agg_cp = send(agg_ref.at[:, other], asib, as_s, as_r, sib_id)
    for ch in range(nch):
        own = gath[ch].at[me_c]
        sib_cp.append(send(own, own, sb_s.at[ch], sb_r.at[ch], sib_id))

    def depart(ch):
        own = gath[ch].at[me_c]
        for way in range(2):
            send_when(has_next[way], lambda way=way: copy(
                own, own, ag_s.at[ch, way, 0], ag_r.at[ch, way, 0], next_id[way]))

    depart(0)

    loads[2].wait()
    agg_cp.wait_recv()
    for ch in range(nch):
        cols = slice(ch * fc, (ch + 1) * fc)
        sib_cp[ch].wait_recv()
        g = dot0(agg_v[...], gath[ch][me_c]) + dot0(asib[...], gath[ch][sib])
        gpart[:, :, cols] = g.astype(BF).reshape(n_row, piece, fc)
    g_cp = [send(gpart.at[(me_r + d) % n_row], grecv.at[d - 1], g_s.at[d - 1], g_r.at[d - 1], row_id(d))
            for d in range(1, n_row)]

    def arrival(way, step):
        src = z - 1 - step if way == 0 else z + 1 + step
        return src, (src >= 0 if way == 0 else src <= n_z - 1)

    def relay(ch, step):
        for way in range(2):
            src, there = arrival(way, step)

            slot = gath[ch].at[src * 2 + core]
            on = there & has_next[way]

            def hop(step, way=way, slot=slot):
                return copy(slot, slot, ag_s.at[ch, way, step], ag_r.at[ch, way, step], next_id[way])

            def over(way=way, slot=slot):
                return copy(slot, slot, fw_s.at[ch, way, step], fw_r.at[ch, way, step], sib_id)

            pl.when(there)(lambda hop=hop: hop(step).wait_recv())
            if step + 1 < n_z - 1:
                send_when(on, functools.partial(hop, step + 1))
            send_when(there, over)

    def gathered(ch):
        for step in range(n_z - 1):
            for way in range(2):
                src, there = arrival(way, step)

                def come(way=way, step=step, src=src):
                    slot = gath[ch].at[src * 2 + 1 - core]
                    copy(slot, slot, fw_s.at[ch, way, step], fw_r.at[ch, way, step], sib_id).wait_recv()

                pl.when(there)(come)

    lanes = 128
    ones = jnp.ones((TILE, n_col * rows), BF)
    bsend[...] = jnp.zeros_like(bsend)

    def contribute(ch):
        gathered(ch)
        if cap == group:
            rhs = jnp.concatenate([gath[ch][pos_ref[0, 0, k] // tbc] for k in range(cap)], axis=0)
            cbuf[ch] = jnp.dot(lhs[...], rhs, preferred_element_type=F32).astype(BF).reshape(n_row, rows, fc)
        else:
            acc_ref = lhs
            acc_ref[...] = jnp.zeros_like(acc_ref)

            def turn(t, carry):
                for i in range(group):
                    k = t * group + i
                    p = pos_ref[0, 0, k]
                    rhs = gath[ch][p // tbc]
                    prod = dot0(blk_v[k], rhs)
                    alive = k < live_ref[0, 0]
                    for j in range(tbc):
                        acc_ref[j * blk:(j + 1) * blk] += jnp.where(alive & (p % tbc == j), prod, 0.0)
                return carry

            lax.fori_loop(0, cap // group, turn, 0)
            cbuf[ch] = acc_ref[...].astype(BF).reshape(n_row, rows, fc)
        cps = [send(cbuf.at[ch, (me_r + d) % n_row], rbuf.at[ch, d - 1], c_s.at[ch, d - 1], c_r.at[ch, d - 1], row_id(d))
               for d in range(1, n_row)]
        return cps

    total = None

    def project(ch, cps):
        for c in cps:
            c.wait_recv()
        s = cbuf[ch, me_r].astype(F32)
        for d in range(1, n_row):
            s += rbuf[ch, d - 1].astype(F32)
        return jnp.dot(s.astype(BF), w_t[ch * fc:(ch + 1) * fc], preferred_element_type=F32)

    def turn_weight():
        loads[4].wait()
        w_t[...] = w_v[...].T

    base = core * half
    at_row = pl.ds(pl.multiple_of(base + me_r * piece, piece), piece)
    at_me = pl.ds(pl.multiple_of(base + me_r * piece + (z * part if scatter else 0), part), part)

    def spread():
        loads[3].wait()
        if cap == group:
            for k in range(cap):
                at = pos_ref[0, 0, k] % tbc
                alive = k < live_ref[0, 0]
                turned = blk_v[k].T
                for j in range(tbc):
                    lhs[j * blk:(j + 1) * blk, k * blk:(k + 1) * blk] = jnp.where(
                        alive & (at == j), turned, jnp.zeros((blk, blk), BF))

    zpick = [zsend.at[(z + d) % n_z if scatter else 0] for d in range(n_z)]
    zz_cp, wz_cp, wr_cp, wf_cp = [], [], [], []

    def row_sum():
        for c in g_cp:
            c.wait_recv()
        acc = gpart[me_r].astype(F32)
        for d in range(1, n_row):
            acc += grecv[d - 1].astype(F32)
        zsend[...] = acc.astype(BF).reshape(zsend.shape)
        for d in range(1, n_z):
            zz_cp.append(send(zpick[d], zrecv.at[d - 1], z_s.at[d - 1], z_r.at[d - 1], z_id(d)))

    def z_sum():
        for c in zz_cp:
            c.wait_recv()
        acc = zpick[0][...].astype(F32)
        for d in range(1, n_z):
            acc += zrecv[d - 1].astype(F32)
        gw[at_me] = acc.astype(BF)
        if scatter:
            for d in range(1, n_z):
                wz_cp.append(send(gw.at[at_me], gw.at[at_me], wz_s.at[d - 1], wz_r.at[d - 1], z_id(d)))

    def row_gather():
        for c in wz_cp:
            c.wait_recv()
        for d in range(1, n_row):
            wr_cp.append(send(gw.at[at_row], gw.at[at_row], wr_s.at[d - 1], wr_r.at[d - 1], row_id(d)))
        wf_cp.append(send(gw.at[at_row], gw.at[at_row], wf_s.at[0], wf_r.at[0], sib_id))

    c_cp = []
    todo = []
    for ch in range(nch):
        at = 1.9 * ch
        if ch >= 1:
            todo.append((at - 1.4, functools.partial(depart, ch)))
        for step in range(n_z - 1):
            todo.append((at + step, functools.partial(relay, ch, step)))
        todo.append((at + n_z - 2 + 0.85, lambda ch=ch: c_cp.append(contribute(ch))))
    todo += [(0.7, spread), (1.6, row_sum), (n_z - 1.5, z_sum), (n_z - 1.05, turn_weight), (n_z - 1.45, row_gather)]
    for _, act in sorted(todo, key=lambda item: item[0]):
        act()

    for ch in range(nch):
        sums = lax.dot_general(ones, gath[ch][...].reshape(n_col * rows, fc), (((1,), (0,)), ((), ())),
                               preferred_element_type=F32)
        for i in range(fc // lanes):
            at = ch * (fc // lanes) + i
            bsend[at:at + 1, :] = sums[0:1, i * lanes:(i + 1) * lanes]
    b_cp = [send(bsend, brecv.at[d - 1], b_s.at[d - 1], b_r.at[d - 1], row_id(d)) for d in range(1, n_row)]

    for ch in range(nch - 1):
        more = project(ch, c_cp[ch])
        total = more if total is None else total + more
    for d in range(1, n_row):
        wr_cp[d - 1].wait_recv()
        src = pl.ds(pl.multiple_of(base + ((me_r + n_row - d) % n_row) * piece, piece), piece)
        wf_cp.append(send(gw.at[src], gw.at[src], wf_s.at[d], wf_r.at[d], sib_id))
    gw_ref[mine] = gw[mine]
    for ch in range(nch - 1, nch):
        more = project(ch, c_cp[ch])
        total = more if total is None else total + more
    gi_ref[...] = total.astype(BF)
    bias = bsend[...]
    for d in range(1, n_row):
        b_cp[d - 1].wait_recv()
        bias += brecv[d - 1]
    gb_ref[...] = bias
    for c in wf_cp:
        c.wait_recv()
    gw_ref[other] = gw[other]
    for now, make in sent:
        if now is None:
            make().wait_send()
        else:
            pl.when(now)(lambda make=make: make().wait_send())


def body(n_row, n_col, grad_out, relu_mask, aggregated, weight, adj_blocks, block_pos, block_live):
    rows, feat = grad_out.shape
    cap, blk = adj_blocks.shape[2], adj_blocks.shape[-1]
    group = max(d for d in range(1, 17) if cap % d == 0)
    nch = 2
    fc = feat // nch
    n_z = n_col // 2
    piece = feat // 2 // n_row
    scatter = False
    part = piece // n_z if scatter else piece
    tbc = n_row * rows // blk
    brows = -(-feat // 1024) * 8
    if cap == group:
        lhs = pltpu.VMEM((tbc * blk, cap * blk), BF)
    else:
        lhs = pltpu.VMEM((tbc * blk, fc), F32)
    dma = pltpu.SemaphoreType.DMA
    scratch = [pltpu.VMEM((n_col, rows, fc), BF) for _ in range(nch)] + [
        lhs,
        pltpu.VMEM((nch, n_row, rows, fc), BF),
        pltpu.VMEM((nch, n_row - 1, rows, fc), BF),
        pltpu.VMEM((rows, feat // 2), BF),
        pltpu.VMEM((n_row, piece, feat), BF),
        pltpu.VMEM((n_row - 1, piece, feat), BF),
        pltpu.VMEM((n_z if scatter else 1, part, feat), BF),
        pltpu.VMEM((n_z - 1, part, feat), BF),
        pltpu.VMEM((feat, feat), BF),
        pltpu.VMEM((rows, feat), BF),
        pltpu.VMEM((rows, feat), jnp.int32),
        pltpu.VMEM((rows, feat // 2), BF),
        pltpu.VMEM((feat, feat), BF),
        pltpu.VMEM((cap, blk, blk), BF),
        pltpu.VMEM((brows, 128), F32),
        pltpu.VMEM((n_row - 1, brows, 128), F32),
        pltpu.VMEM((feat, feat), BF),
    ]
    sems = [dma((nch, 2, n_z - 1)), dma((nch, 2, n_z - 1)), dma((nch, 2, n_z - 1)), dma((nch, 2, n_z - 1)),
            dma((nch, n_row - 1)), dma((nch, n_row - 1)), dma(()), dma(()),
            dma((n_row - 1,)), dma((n_row - 1,)), dma((n_z - 1,)), dma((n_z - 1,)),
            dma((n_z - 1,)), dma((n_z - 1,)), dma((n_row - 1,)), dma((n_row - 1,)),
            dma((n_row,)), dma((n_row,)), dma((n_row - 1,)), dma((n_row - 1,)), dma((5,)),
            dma((nch,)), dma((nch,))]
    vm = pl.BlockSpec(memory_space=pltpu.VMEM)
    hbm = pl.BlockSpec(memory_space=pltpu.HBM)
    sm = pl.BlockSpec(memory_space=pltpu.SMEM)
    gi, gw, gb = pl.pallas_call(
        functools.partial(kernel, (n_row, n_col, nch, cap, group, scatter)),
        out_shape=(jax.ShapeDtypeStruct((rows, feat), BF),
                   jax.ShapeDtypeStruct((feat, feat), BF),
                   jax.ShapeDtypeStruct((brows, 128), F32)),
        in_specs=[hbm, hbm, hbm, hbm, hbm, sm, sm],
        out_specs=(vm, vm, vm),
        scratch_shapes=scratch + sems,
        compiler_params=pltpu.CompilerParams(collective_id=0, has_side_effects=True,
                                             vmem_limit_bytes=(8 if cap == group else 48) * 1024 * 1024),
    )(*(pltpu.with_memory_space_constraint(x, pltpu.HBM)
        for x in (grad_out, relu_mask, aggregated, weight, adj_blocks)), block_pos, block_live)
    factor = 1.0 / math.sqrt(rows * n_row * n_col)
    return gi.reshape(1, rows, feat), gw.astype(F32) * factor, gb.reshape(-1)[:feat] * factor


def solution(mesh):
    return jax.shard_map(
        functools.partial(body, mesh.shape["row"], mesh.shape["col"]),
        mesh=mesh,
        in_specs=(
            P(("row", "col"), None),
            P(("row", "col"), None),
            P(("row", "col"), None),
            P(),
            P("row", "col", None, None, None),
            P("row", "col", None),
            P("row", "col"),
        ),
        out_specs=(P("col", "row", None), P(), P()),
        check_vma=False,
    )
```

```python
import functools
import math

import jax
import jax.numpy as jnp
from jax import lax
from jax.experimental import pallas as pl
from jax.experimental.pallas import tpu as pltpu
from jax.sharding import PartitionSpec as P

MESH = pl.DeviceIdType.MESH
BF = jnp.bfloat16
F32 = jnp.float32
TILE = 16


def dot0(a, b):
    return lax.dot_general(a, b, (((0,), (0,)), ((), ())), preferred_element_type=F32)


def kernel(cfg, go_ref, mask_ref, agg_ref, w_ref, blk_ref, pos_ref, live_ref,
           gi_ref, gw_ref, gb_ref, *scr):
    n_row, n_col, nch, cap, group, scatter = cfg
    n_z = n_col // 2
    gath = scr[:nch]
    lhs, cbuf, rbuf, asib, gpart, grecv, zsend, zrecv, gw, go_v, mask_v, agg_v, w_v, blk_v, bsend, brecv, w_t = scr[nch:nch + 17]
    (ag_s, ag_r, fw_s, fw_r, c_s, c_r, as_s, as_r, g_s, g_r, z_s, z_r, wz_s, wz_r, wr_s, wr_r, wf_s, wf_r,
     b_s, b_r, in_s, sb_s, sb_r) = scr[nch + 17:]
    rows, feat = go_ref.shape
    fc = feat // nch
    blk = blk_ref.shape[-1]
    tbc = n_row * rows // blk
    half = feat // 2
    piece = half // n_row
    part = piece // n_z if scatter else piece
    me_r, me_c = lax.axis_index("row"), lax.axis_index("col")
    z, core = me_c // 2, me_c % 2
    sib = z * 2 + 1 - core
    sib_id = (me_r, sib)

    def row_id(d):
        return ((me_r + d) % n_row, me_c)

    def z_id(d):
        return (me_r, ((z + d) % n_z) * 2 + core)

    other = pl.ds(pl.multiple_of((1 - core) * half, half), half)
    mine = pl.ds(pl.multiple_of(core * half, half), half)
    loads = [pltpu.make_async_copy(src, dst, in_s.at[i]) for i, (src, dst) in enumerate((
        (go_ref, go_v), (mask_ref, mask_v), (agg_ref.at[:, mine], agg_v), (blk_ref.at[0, 0], blk_v), (w_ref, w_v)))]
    for c in loads:
        c.start()

    sent = []

    def copy(src, dst, s, r, dev):
        return pltpu.make_async_remote_copy(src_ref=src, dst_ref=dst, send_sem=s, recv_sem=r,
                                               device_id=dev, device_id_type=MESH)

    def send(*what):
        c = copy(*what)
        c.start()
        sent.append((None, lambda: copy(*what)))
        return c

    def send_when(now, make):
        pl.when(now)(lambda: make().start())
        sent.append((now, make))

    barrier = pltpu.get_barrier_semaphore()
    peers = [sib_id] + [z_id(d) for d in range(1, n_z)] + [row_id(d) for d in range(1, n_row)]
    for p in peers:
        pl.semaphore_signal(barrier, inc=1, device_id=p, device_id_type=MESH)

    loads[0].wait()
    loads[1].wait()
    for ch in range(nch):
        cols = slice(ch * fc, (ch + 1) * fc)
        gath[ch][me_c] = go_v[:, cols] * mask_v[:, cols].astype(F32).astype(BF)

    pl.semaphore_wait(barrier, len(peers))

    has_next = (z < n_z - 1, z > 0)
    next_id = ((me_r, me_c + 2), (me_r, me_c - 2))
    sib_cp = []
    agg_cp = send(agg_ref.at[:, other], asib, as_s, as_r, sib_id)
    for ch in range(nch):
        own = gath[ch].at[me_c]
        sib_cp.append(send(own, own, sb_s.at[ch], sb_r.at[ch], sib_id))

    def depart(ch):
        own = gath[ch].at[me_c]
        for way in range(2):
            send_when(has_next[way], lambda way=way: copy(
                own, own, ag_s.at[ch, way, 0], ag_r.at[ch, way, 0], next_id[way]))

    depart(0)

    loads[2].wait()
    agg_cp.wait_recv()
    for ch in range(nch):
        cols = slice(ch * fc, (ch + 1) * fc)
        sib_cp[ch].wait_recv()
        g = dot0(agg_v[...], gath[ch][me_c]) + dot0(asib[...], gath[ch][sib])
        gpart[:, :, cols] = g.astype(BF).reshape(n_row, piece, fc)
    g_cp = [send(gpart.at[(me_r + d) % n_row], grecv.at[d - 1], g_s.at[d - 1], g_r.at[d - 1], row_id(d))
            for d in range(1, n_row)]

    def arrival(way, step):
        src = z - 1 - step if way == 0 else z + 1 + step
        return src, (src >= 0 if way == 0 else src <= n_z - 1)

    def relay(ch, step):
        for way in range(2):
            src, there = arrival(way, step)

            slot = gath[ch].at[src * 2 + core]
            on = there & has_next[way]

            def hop(step, way=way, slot=slot):
                return copy(slot, slot, ag_s.at[ch, way, step], ag_r.at[ch, way, step], next_id[way])

            def over(way=way, slot=slot):
                return copy(slot, slot, fw_s.at[ch, way, step], fw_r.at[ch, way, step], sib_id)

            pl.when(there)(lambda hop=hop: hop(step).wait_recv())
            if step + 1 < n_z - 1:
                send_when(on, functools.partial(hop, step + 1))
            send_when(there, over)

    def gathered(ch):
        for step in range(n_z - 1):
            for way in range(2):
                src, there = arrival(way, step)

                def come(way=way, step=step, src=src):
                    slot = gath[ch].at[src * 2 + 1 - core]
                    copy(slot, slot, fw_s.at[ch, way, step], fw_r.at[ch, way, step], sib_id).wait_recv()

                pl.when(there)(come)

    lanes = 128
    ones = jnp.ones((TILE, n_col * rows), BF)
    bsend[...] = jnp.zeros_like(bsend)

    def contribute(ch):
        gathered(ch)
        if cap == group:
            rhs = jnp.concatenate([gath[ch][pos_ref[0, 0, k] // tbc] for k in range(cap)], axis=0)
            cbuf[ch] = jnp.dot(lhs[...], rhs, preferred_element_type=F32).astype(BF).reshape(n_row, rows, fc)
        else:
            acc_ref = lhs
            acc_ref[...] = jnp.zeros_like(acc_ref)

            def turn(t, carry):
                for i in range(group):
                    k = t * group + i
                    p = pos_ref[0, 0, k]
                    rhs = gath[ch][p // tbc]
                    prod = dot0(blk_v[k], rhs)
                    alive = k < live_ref[0, 0]
                    for j in range(tbc):
                        acc_ref[j * blk:(j + 1) * blk] += jnp.where(alive & (p % tbc == j), prod, 0.0)
                return carry

            lax.fori_loop(0, cap // group, turn, 0)
            cbuf[ch] = acc_ref[...].astype(BF).reshape(n_row, rows, fc)
        cps = [send(cbuf.at[ch, (me_r + d) % n_row], rbuf.at[ch, d - 1], c_s.at[ch, d - 1], c_r.at[ch, d - 1], row_id(d))
               for d in range(1, n_row)]
        return cps

    total = None

    def project(ch, cps):
        for c in cps:
            c.wait_recv()
        s = cbuf[ch, me_r].astype(F32)
        for d in range(1, n_row):
            s += rbuf[ch, d - 1].astype(F32)
        return jnp.dot(s.astype(BF), w_t[ch * fc:(ch + 1) * fc], preferred_element_type=F32)

    def turn_weight():
        loads[4].wait()
        w_t[...] = w_v[...].T

    base = core * half
    at_row = pl.ds(pl.multiple_of(base + me_r * piece, piece), piece)
    at_me = pl.ds(pl.multiple_of(base + me_r * piece + (z * part if scatter else 0), part), part)

    def spread():
        loads[3].wait()
        if cap == group:
            for k in range(cap):
                at = pos_ref[0, 0, k] % tbc
                alive = k < live_ref[0, 0]
                turned = blk_v[k].T
                for j in range(tbc):
                    lhs[j * blk:(j + 1) * blk, k * blk:(k + 1) * blk] = jnp.where(
                        alive & (at == j), turned, jnp.zeros((blk, blk), BF))

    zpick = [zsend.at[(z + d) % n_z if scatter else 0] for d in range(n_z)]
    zz_cp, wz_cp, wr_cp, wf_cp = [], [], [], []

    def row_sum():
        for c in g_cp:
            c.wait_recv()
        acc = gpart[me_r].astype(F32)
        for d in range(1, n_row):
            acc += grecv[d - 1].astype(F32)
        zsend[...] = acc.astype(BF).reshape(zsend.shape)
        for d in range(1, n_z):
            zz_cp.append(send(zpick[d], zrecv.at[d - 1], z_s.at[d - 1], z_r.at[d - 1], z_id(d)))

    def z_sum():
        for c in zz_cp:
            c.wait_recv()
        acc = zpick[0][...].astype(F32)
        for d in range(1, n_z):
            acc += zrecv[d - 1].astype(F32)
        gw[at_me] = acc.astype(BF)
        if scatter:
            for d in range(1, n_z):
                wz_cp.append(send(gw.at[at_me], gw.at[at_me], wz_s.at[d - 1], wz_r.at[d - 1], z_id(d)))

    def row_gather():
        for c in wz_cp:
            c.wait_recv()
        for d in range(1, n_row):
            wr_cp.append(send(gw.at[at_row], gw.at[at_row], wr_s.at[d - 1], wr_r.at[d - 1], row_id(d)))
        wf_cp.append(send(gw.at[at_row], gw.at[at_row], wf_s.at[0], wf_r.at[0], sib_id))

    def bias_sum(ch):
        sums = lax.dot_general(ones, gath[ch][...].reshape(n_col * rows, fc), (((1,), (0,)), ((), ())),
                               preferred_element_type=F32)
        for i in range(fc // lanes):
            at = ch * (fc // lanes) + i
            bsend[at:at + 1, :] = sums[0:1, i * lanes:(i + 1) * lanes]

    c_cp = []
    todo = []
    for ch in range(nch):
        at = 1.9 * ch
        if ch >= 1:
            todo.append((at - 1.4, functools.partial(depart, ch)))
        for step in range(n_z - 1):
            todo.append((at + step, functools.partial(relay, ch, step)))
        todo.append((at + n_z - 2 + 0.85, lambda ch=ch: c_cp.append(contribute(ch))))
        todo.append((at + n_z - 2 + 0.87, functools.partial(bias_sum, ch)))
    todo += [(0.7, spread), (1.6, row_sum), (n_z - 1.5, z_sum), (n_z - 1.05, turn_weight), (n_z - 0.5, row_gather)]
    for _, act in sorted(todo, key=lambda item: item[0]):
        act()

    b_cp = [send(bsend, brecv.at[d - 1], b_s.at[d - 1], b_r.at[d - 1], row_id(d)) for d in range(1, n_row)]

    for ch in range(nch - 1):
        more = project(ch, c_cp[ch])
        total = more if total is None else total + more
    for d in range(1, n_row):
        wr_cp[d - 1].wait_recv()
        src = pl.ds(pl.multiple_of(base + ((me_r + n_row - d) % n_row) * piece, piece), piece)
        wf_cp.append(send(gw.at[src], gw.at[src], wf_s.at[d], wf_r.at[d], sib_id))
    gw_ref[mine] = gw[mine]
    for ch in range(nch - 1, nch):
        more = project(ch, c_cp[ch])
        total = more if total is None else total + more
    gi_ref[...] = total.astype(BF)
    bias = bsend[...]
    for d in range(1, n_row):
        b_cp[d - 1].wait_recv()
        bias += brecv[d - 1]
    gb_ref[...] = bias
    for c in wf_cp:
        c.wait_recv()
    gw_ref[other] = gw[other]
    for now, make in sent:
        if now is None:
            make().wait_send()
        else:
            pl.when(now)(lambda make=make: make().wait_send())


def body(n_row, n_col, grad_out, relu_mask, aggregated, weight, adj_blocks, block_pos, block_live):
    rows, feat = grad_out.shape
    cap, blk = adj_blocks.shape[2], adj_blocks.shape[-1]
    group = max(d for d in range(1, 17) if cap % d == 0)
    nch = 2
    fc = feat // nch
    n_z = n_col // 2
    piece = feat // 2 // n_row
    scatter = piece % (n_z * TILE) == 0
    part = piece // n_z if scatter else piece
    tbc = n_row * rows // blk
    brows = -(-feat // 1024) * 8
    if cap == group:
        lhs = pltpu.VMEM((tbc * blk, cap * blk), BF)
    else:
        lhs = pltpu.VMEM((tbc * blk, fc), F32)
    dma = pltpu.SemaphoreType.DMA
    scratch = [pltpu.VMEM((n_col, rows, fc), BF) for _ in range(nch)] + [
        lhs,
        pltpu.VMEM((nch, n_row, rows, fc), BF),
        pltpu.VMEM((nch, n_row - 1, rows, fc), BF),
        pltpu.VMEM((rows, feat // 2), BF),
        pltpu.VMEM((n_row, piece, feat), BF),
        pltpu.VMEM((n_row - 1, piece, feat), BF),
        pltpu.VMEM((n_z if scatter else 1, part, feat), BF),
        pltpu.VMEM((n_z - 1, part, feat), BF),
        pltpu.VMEM((feat, feat), BF),
        pltpu.VMEM((rows, feat), BF),
        pltpu.VMEM((rows, feat), jnp.int32),
        pltpu.VMEM((rows, feat // 2), BF),
        pltpu.VMEM((feat, feat), BF),
        pltpu.VMEM((cap, blk, blk), BF),
        pltpu.VMEM((brows, 128), F32),
        pltpu.VMEM((n_row - 1, brows, 128), F32),
        pltpu.VMEM((feat, feat), BF),
    ]
    sems = [dma((nch, 2, n_z - 1)), dma((nch, 2, n_z - 1)), dma((nch, 2, n_z - 1)), dma((nch, 2, n_z - 1)),
            dma((nch, n_row - 1)), dma((nch, n_row - 1)), dma(()), dma(()),
            dma((n_row - 1,)), dma((n_row - 1,)), dma((n_z - 1,)), dma((n_z - 1,)),
            dma((n_z - 1,)), dma((n_z - 1,)), dma((n_row - 1,)), dma((n_row - 1,)),
            dma((n_row,)), dma((n_row,)), dma((n_row - 1,)), dma((n_row - 1,)), dma((5,)),
            dma((nch,)), dma((nch,))]
    vm = pl.BlockSpec(memory_space=pltpu.VMEM)
    hbm = pl.BlockSpec(memory_space=pltpu.HBM)
    sm = pl.BlockSpec(memory_space=pltpu.SMEM)
    gi, gw, gb = pl.pallas_call(
        functools.partial(kernel, (n_row, n_col, nch, cap, group, scatter)),
        out_shape=(jax.ShapeDtypeStruct((rows, feat), BF),
                   jax.ShapeDtypeStruct((feat, feat), BF),
                   jax.ShapeDtypeStruct((brows, 128), F32)),
        in_specs=[hbm, hbm, hbm, hbm, hbm, sm, sm],
        out_specs=(vm, vm, vm),
        scratch_shapes=scratch + sems,
        compiler_params=pltpu.CompilerParams(collective_id=0, has_side_effects=True,
                                             vmem_limit_bytes=(8 if cap == group else 48) * 1024 * 1024),
    )(*(pltpu.with_memory_space_constraint(x, pltpu.HBM)
        for x in (grad_out, relu_mask, aggregated, weight, adj_blocks)), block_pos, block_live)
    factor = 1.0 / math.sqrt(rows * n_row * n_col)
    return gi.reshape(1, rows, feat), gw.astype(F32) * factor, gb.reshape(-1)[:feat] * factor


def solution(mesh):
    return jax.shard_map(
        functools.partial(body, mesh.shape["row"], mesh.shape["col"]),
        mesh=mesh,
        in_specs=(
            P(("row", "col"), None),
            P(("row", "col"), None),
            P(("row", "col"), None),
            P(),
            P("row", "col", None, None, None),
            P("row", "col", None),
            P("row", "col"),
        ),
        out_specs=(P("col", "row", None), P(), P()),
        check_vma=False,
    )
```
